32 devices in a mesh: groups: 2 (over x), tx: 16 (over z, y, core).
Axes of the slice: x: 2, y: 2, z: 4, core: 2. Of those that a mesh axis runs over, the one named last changes fastest.
Arguments:
- voltage: float32 [256, 16, 1024], P(('groups', 'tx')), parts along dimension 0, may hold values from -3 to 3
- gating: float32 [256, 16, 1024], P(('groups', 'tx')), parts along dimension 0, may hold values from 0.05 to 0.95
- recovery: float32 [256, 16, 1024], P(('groups', 'tx')), parts along dimension 0, may hold values from -3 to 3
- tangents: float32 [8, 3, 256, 16, 1024], P(None, None, ('groups', 'tx')), parts along dimension 2, may hold values from -6 to 6
- parameters: float32 [16], P('groups'), parts along dimension 0, may hold values from 0.5 to 2
- region: int32 [256, 16, 1024], P(('groups', 'tx')), parts along dimension 0, may hold values from 0 to 7
- fiber_class: int32 [256, 16, 1024], P(('groups', 'tx')), parts along dimension 0, may hold values from 0 to 3
- electrode_site: int32 [8192], P(('groups', 'tx')), parts along dimension 0, may hold values from 0 to 8191
- electrode_owner: int32 [8192, 1], P(('groups', 'tx')), parts along dimension 0, may hold values from 0 to 15; in each aligned block of 256 rows (0 to 255, 256 to 511, ...) at most 16 rows name the same one
Outputs:
- tangents_out: float32 [8, 3, 256, 16, 1024], P(None, None, ('groups', 'tx')), parts along dimension 2
- jacobian: float32 [8192, 128], P(('groups', 'tx')), parts along dimension 0
The draws below stay inside these ranges and needn't reach their ends.
There are 2 independent parts, one for each index of `groups`. The reference program is written for one: setup_inputs(seed, part) draws one part's arguments, and reference() takes and returns one part's arrays. A program takes and returns all parts, laid end to end along the dimension named above; each array names one. Nothing has to cross between parts.
Inputs may be any that keep to these rules, and one draw needn't show every extreme that they name: `electrode_owner`: among the electrodes of one tile at most 16 have the same owner, and in every draw some tile sends exactly 16 to one owner.
All inputs are finite; a program needn't handle non-finite values.
Results may differ from the reference program's by a relative error of at most 0.00002.
Values sent between devices are 32-bit elements; how exact they have to be, the bound alone decides.
No kernel may reach another device: no remote copies, remote signals or barrier semaphores. Data moves between devices by JAX's collectives and lax.ppermute only.
A program may use at most 192 MiB of HBM per device.

```python
import math
import jax
import jax.numpy as jnp
import numpy as np

P_SIZE = 8
NZ = 16
NY = 1024
CX = 8
E_DEV = 256
CAP = 16
NX = 128
ELECTRODES = 4096
N_TX = 16


def place_ends(result, own_key, low, top_value):
    shape = result.shape
    index_at = [jax.random.randint(jax.random.fold_in(own_key, axis), (), 0, shape[axis]) for axis in range(len(shape))]
    result = result.at[tuple(index_at)].set(low)
    longest = shape.index(max(shape))
    index_at[longest] = (index_at[longest] + 1) % shape[longest]
    return result.at[tuple(index_at)].set(top_value)


def level_of(stream_key, shape, shards, smallest, high):
    gain = 1.0
    for axis_at, parts in shards:
        heights = jax.random.uniform(jax.random.fold_in(jax.random.fold_in(stream_key, 6), axis_at), (parts,), jnp.float32, smallest / len(shards), high / len(shards))
        gain = gain * jnp.repeat(jnp.exp(heights), shape[axis_at] // parts).reshape((-1,) + (1,) * (len(shape) - 1 - axis_at))
    return gain


def assign_block(key, own, number, rows, number_of, top, limit, skew):
    sequence = jax.random.permutation(key, number_of)
    crowded, ordinary = portions_of(number_of, rows * top, limit, skew, True), portions_of(number_of, rows * top, limit, skew, False)
    places = jnp.arange(number_of)

    def named(tallies, offset_by):
        used = int((tallies > 0).sum())
        fixed = max(1, used // 4)
        passed = fixed + (places - fixed + offset_by * (used - fixed)) % max(1, number_of - fixed)
        return jnp.zeros((number_of,), jnp.int32).at[sequence[jnp.where(places < fixed, places, passed)]].set(jnp.asarray(tallies, jnp.int32))

    tallies = jnp.where(number % 4 == 0, named(crowded, number // 4), named(ordinary, number - number // 4 - 1))
    mixed = jax.random.permutation(jax.random.fold_in(own, 3), number_of)
    donor, sink = mixed[0:number_of // 2 * 2:2], mixed[1:number_of // 2 * 2:2]
    room = jnp.minimum(tallies[donor] - 1, limit - tallies[sink]) // 2
    room = jnp.where((donor == sequence[0]) | (sink == sequence[0]) | (tallies[sink] == 0), 0, jnp.maximum(room, 0))
    passed = jax.random.randint(jax.random.fold_in(own, 4), (number_of // 2,), 0, 1 << 20) % (room + 1)
    tallies = tallies.at[donor].add(-passed).at[sink].add(passed)
    items = jnp.searchsorted(jnp.cumsum(tallies), jnp.arange(rows * top), side="right").astype(jnp.int32)
    listing = items.reshape(top, rows).T
    listing = listing[jax.random.permutation(jax.random.fold_in(own, 1), rows)]
    offset_by = jax.random.randint(jax.random.fold_in(own, 2), (rows, 1), 0, top)
    return jnp.take_along_axis(listing, (jnp.arange(top)[None, :] + offset_by) % top, axis=1)


def portions_of(number_of, total, bound, skew, full):
    weights = [(1 << 20) // math.isqrt(rank ** skew) + 1 for rank in range(1, number_of + 1)]
    largest = bound if full else min(bound, max(-(-total // number_of), total * weights[0] // sum(weights)))
    least = 1 if total - largest >= number_of - 1 else 0
    given, rest = [largest] + [least] * (number_of - 1), total - largest - least * (number_of - 1)
    while rest > 0:
        free = [i for i in range(1, number_of) if given[i] < largest] or [i for i in range(1, number_of) if given[i] < bound]
        pool, left = sum([weights[i] for i in free]), rest
        for i in free:
            extra = min(bound - given[i], max(1, left * weights[i] // pool), rest)
            given[i] = given[i] + extra
            rest = rest - extra
    return np.array(given)


def scatter_about(own_key, extent, width, reach, pieces=(), held_as=jnp.bfloat16):
    level = level_of(own_key, extent, pieces, -0.22, 0.18) if pieces else 1.0
    drawn = jax.random.normal(own_key, extent, jnp.float32) * width * level
    return jnp.minimum(jnp.maximum(drawn, -reach), reach).astype(held_as)


def setup_inputs(seed: int = 0, part: int = 0) -> dict:
    splits = jax.random.split(jax.random.key(seed), 10)
    part_splits = jax.random.split(jax.random.fold_in(splits[9], part), 10)
    voltage = scatter_about(part_splits[0], (NX, NZ, NY), 1.0, 3.0, ((0, 16),), jnp.float32)
    gating = jnp.clip(0.05 + 0.9 * jax.random.uniform(part_splits[1], (NX, NZ, NY), jnp.float32) ** level_of(part_splits[1], (NX, NZ, NY), ((0, 16),), -0.2, 0.2), 0.05, 0.95)
    recovery = scatter_about(part_splits[2], (NX, NZ, NY), 0.5, 3.0, ((0, 16),), jnp.float32)
    tangents = scatter_about(part_splits[3], (P_SIZE, 3, NX, NZ, NY), 1.0, 6.0, ((2, 16),), jnp.float32)
    parameters = jnp.clip(jnp.exp(jax.random.uniform(part_splits[4], (P_SIZE,), jnp.float32, math.log(0.5), math.log(2.0))), 0.5, 2.0)
    region = place_ends(jax.random.randint(part_splits[5], (NX, NZ, NY), 0, P_SIZE), jax.random.fold_in(part_splits[5], 1), 0, P_SIZE - 1).astype(jnp.int32)
    fiber_class = place_ends(jax.random.randint(part_splits[6], (NX, NZ, NY), 0, 4), jax.random.fold_in(part_splits[6], 1), 0, 3).astype(jnp.int32)
    electrode_site = place_ends(jax.random.randint(part_splits[7], (ELECTRODES,), 0, CX * NY), jax.random.fold_in(part_splits[7], 1), 0, (CX * NY) - 1).astype(jnp.int32)
    electrode_owner_keys = jax.random.split(jax.random.fold_in(part_splits[8], 1), ELECTRODES // E_DEV)
    electrode_owner_turns = jax.random.permutation(jax.random.fold_in(part_splits[8], 3), ELECTRODES // E_DEV)
    electrode_owner = jax.vmap(lambda own, number: assign_block(jax.random.fold_in(part_splits[8], 2), own, number, E_DEV, N_TX, 1, CAP, 2))(electrode_owner_keys, electrode_owner_turns).reshape((ELECTRODES, 1))
    return dict(voltage=voltage, gating=gating, recovery=recovery, tangents=tangents, parameters=parameters, region=region, fiber_class=fiber_class, electrode_site=electrode_site, electrode_owner=electrode_owner)


TIME_STEP = 0.1
ION_SCALE = 2.0
GATE_RATE = 0.25
RECOVERY_RATE = 0.5
RECOVERY_DECAY = 0.8
COND_ALONG = 1.0
COND_ACROSS = 0.25
COND_DEPTH = 0.25
GATE_STEEP = 4.0


def conduct(fiber_class):
    along = jnp.where(fiber_class == 0, 1.0, jnp.where(fiber_class == 2, 0.0, 0.5)).astype(jnp.float32)
    oblique = jnp.where(fiber_class == 1, 0.5, jnp.where(fiber_class == 3, -0.5, 0.0)).astype(jnp.float32)
    spread_gap = COND_ALONG - COND_ACROSS
    return (COND_ACROSS + spread_gap * along, COND_ACROSS + spread_gap * (1.0 - along), spread_gap * oblique)


def regional(region, parameters):
    labels = jnp.arange(parameters.shape[0], dtype=jnp.int32)
    member = (region[None] == labels[:, None, None, None]).astype(jnp.float32)
    return member, jnp.sum(member * parameters[:, None, None, None], axis=0)


def spread(padded, coeffs):
    coef_xx, coef_yy, coef_xy = coeffs
    zeros_y = [(0, 0)] * (padded.ndim - 1) + [(1, 1)]
    y_padded = jnp.pad(padded, zeros_y)
    centre = padded[..., 1:-1, :, :]
    along_x = y_padded[..., 2:, :, 1:-1] - 2.0 * centre + y_padded[..., :-2, :, 1:-1]
    along_y = y_padded[..., 1:-1, :, 2:] - 2.0 * centre + y_padded[..., 1:-1, :, :-2]
    cross_xy = y_padded[..., 2:, :, 2:] - y_padded[..., 2:, :, :-2] - y_padded[..., :-2, :, 2:] + y_padded[..., :-2, :, :-2]
    z_above = jnp.concatenate([centre[..., 1:, :], centre[..., -1:, :]], axis=-2)
    z_below = jnp.concatenate([centre[..., :1, :], centre[..., :-1, :]], axis=-2)
    along_z = z_above - 2.0 * centre + z_below
    return coef_xx * along_x + coef_yy * along_y + 0.5 * coef_xy * cross_xy + COND_DEPTH * along_z


def advance(stacked, gating, recovery, tan_h, tan_c, coeffs, member, local_gain):
    diffusion = spread(stacked, coeffs)
    potential = stacked[0, 1:-1]
    tan_v = stacked[1:, 1:-1]
    current = potential - potential * potential * potential / 3.0
    current_slope = 1.0 - potential * potential
    gate_target = jax.nn.sigmoid(GATE_STEEP * potential)
    gate_slope = GATE_STEEP * gate_target * (1.0 - gate_target)
    ionic_gain = ION_SCALE * local_gain
    potential_new = potential + TIME_STEP * (diffusion[0] + ionic_gain * gating * current - recovery)
    gating_new = gating + GATE_RATE * (gate_target - gating)
    recovery_new = recovery + TIME_STEP * RECOVERY_RATE * (potential - RECOVERY_DECAY * recovery)
    tan_v_new = tan_v + TIME_STEP * (diffusion[1:] + ionic_gain * (gating * current_slope * tan_v + current * tan_h)
                                     + ION_SCALE * member * gating * current - tan_c)
    tan_h_new = tan_h + GATE_RATE * (gate_slope * tan_v - tan_h)
    tan_c_new = tan_c + TIME_STEP * RECOVERY_RATE * (tan_v - RECOVERY_DECAY * tan_c)
    return potential_new, gating_new, recovery_new, tan_v_new, tan_h_new, tan_c_new


def reference(voltage, gating, recovery, tangents, parameters, region, fiber_class, electrode_site, electrode_owner):
    coeffs = conduct(fiber_class)
    member, local_gain = regional(region, parameters)
    tan_v = tangents[:, 0]
    tan_h = tangents[:, 1]
    tan_c = tangents[:, 2]
    for repeat in range(2):
        stacked = jnp.concatenate([voltage[None], tan_v], axis=0)
        stacked = jnp.pad(stacked, ((0, 0), (1, 1), (0, 0), (0, 0)))
        voltage, gating, recovery, tan_v, tan_h, tan_c = advance(stacked, gating, recovery, tan_h, tan_c, coeffs, member, local_gain)
    tangents_out = jnp.stack([tan_v, tan_h, tan_c], axis=1)
    owners = electrode_owner[:, 0].reshape(N_TX, E_DEV)
    chosen = (owners[:, :, None] == jnp.arange(N_TX, dtype=jnp.int32)[None, None, :]).astype(jnp.int32)
    slot_rank = jnp.sum((jnp.cumsum(chosen, axis=1) - 1) * chosen, axis=2)
    source = jnp.arange(N_TX, dtype=jnp.int32)[:, None]
    target = (owners * (N_TX * CAP) + source * CAP + slot_rank).reshape(-1).astype(jnp.int32)
    probe_sites = electrode_site.reshape(N_TX, E_DEV)
    column_x = (source * CX + probe_sites // NY).reshape(-1).astype(jnp.int32)
    column_y = (probe_sites % NY).reshape(-1).astype(jnp.int32)
    probe_rows = tan_v[:, column_x, :, column_y]
    probe_rows = probe_rows.reshape(probe_rows.shape[0], P_SIZE * NZ)
    jacobian = jnp.zeros((N_TX * N_TX * CAP, P_SIZE * NZ), jnp.float32).at[target].set(probe_rows)
    return tangents_out, jacobian
```

```python
import functools

import jax
import jax.numpy as jnp
from jax import lax
from jax.experimental import pallas as pl
from jax.experimental.pallas import tpu as pltpu
from jax.sharding import PartitionSpec as P

CAP = 16
LANES = 128
MIB = 1 << 20

CENTRE = 0.7
DEPTH = 0.025


def rolled(x, shift, axis):
    return pltpu.roll(x, shift % x.shape[axis], axis)


def stencil_coeffs(fiber):
    width = fiber.shape[-1]
    x_coef = jnp.where(fiber == 0, 0.1, jnp.where(fiber == 2, 0.025, 0.0625))
    y_coef = 0.125 - x_coef
    w_coef = jnp.where(fiber == 1, 0.01875, jnp.where(fiber == 3, -0.01875, 0.0))
    return (x_coef,) + shifted_pair(y_coef, width) + shifted_pair(w_coef, width)


def shifted_pair(coef, width):
    lane = lax.broadcasted_iota(jnp.int32, coef.shape, 1)
    before = jnp.where(lane == 0, 0.0, rolled(coef, 1, 1))
    after = jnp.where(lane == width - 1, 0.0, rolled(coef, -1, 1))
    return before, after


def depth_sum(u):
    level = lax.broadcasted_iota(jnp.int32, u.shape, 0)
    below = jnp.where(level == 0, u, rolled(u, 1, 0))
    above = jnp.where(level == u.shape[0] - 1, u, rolled(u, -1, 0))
    return below + above


def plane(u, low, high, coeffs):
    x_coef, y_before, y_after, w_before, w_after = coeffs
    if low is None:
        total, gap = high, high
    elif high is None:
        total, gap = low, -low
    else:
        total, gap = low + high, high - low
    return (
        x_coef * total
        + rolled(y_before * u + w_before * gap, -1, 1)
        + rolled(y_after * u - w_after * gap, 1, 1)
    )


def one_sided(u, sign, x_coef, w_before, w_after):
    part = rolled(w_before * u, -1, 1) - rolled(w_after * u, 1, 1)
    return x_coef * u + part if sign > 0 else x_coef * u - part


def local_gain(region, params):
    gain = jnp.zeros(region.shape, jnp.float32)
    for p in range(params.shape[0]):
        gain = jnp.where(region == p, params[p], gain)
    return 0.2 * gain


def reaction(v, h, gain):
    current = v - v * v * v * (1.0 / 3.0)
    slope = 1.0 - v * v
    gate = 1.0 / (1.0 + jnp.exp(-4.0 * v))
    of_v = CENTRE + gain * h * slope
    return of_v, gain * current, 0.2 * h * current, gate * (1.0 - gate), gate, gain * h * current


def edges_kernel(tan, v, left, right, sems):
    fields = tan.shape[0]
    last = tan.shape[2] - 1
    copies = []
    for k, (row, out) in enumerate(((0, left), (last, right))):
        copies.append(pltpu.make_async_copy(tan.at[:, 0, row], out.at[pl.ds(0, fields)], sems.at[2 * k]))
        copies.append(pltpu.make_async_copy(v.at[row], out.at[fields], sems.at[2 * k + 1]))
    for copy in copies:
        copy.start()
    for copy in copies:
        copy.wait()


def partial_kernel(params, *refs):
    ins, (left, right), coef = refs[:10], refs[10:12], refs[12]
    chunk = ins[0].shape[0]
    step = pl.program_id(0)
    for side, out in ((0, left), (1, right)):
        tan, v, h, reg, fib = ins[5 * side : 5 * side + 5]
        outer, inner = (0, 1) if side == 0 else (1, 0)

        @pl.when(step == 0)
        def _():
            fiber = fib[outer]
            of_v, of_h, of_m, _, _, _ = reaction(v[outer], h[outer], local_gain(reg[outer], params))
            for i, value in enumerate(stencil_coeffs(fiber) + (of_v, of_h, of_m)):
                coef[side, i] = value
            out[out.shape[0] - 1] = (fiber + 1).astype(jnp.float32)

        for j in range(chunk):
            p = step * chunk + j
            u, other = tan[j, 0, outer], tan[j, 0, inner]
            coeffs = tuple(coef[side, i] for i in range(5))
            low, high = (None, other) if side == 0 else (other, None)
            out[p] = (
                coef[side, 5] * u
                + plane(u, low, high, coeffs)
                + DEPTH * depth_sum(u)
                + coef[side, 6] * tan[j, 1, outer]
                + jnp.where(reg[outer] == p, coef[side, 7], 0.0)
                - 0.1 * tan[j, 2, outer]
            )


def main_kernel(params, v, h, c, reg, fib, tan, out, near, coef, gate_1, gate_2, dv, dh, dc):
    p = pl.program_id(0)
    rows = v.shape[0]

    def each_row(body):
        body(0, True, False)
        pl.loop(1, rows - 1)(lambda x: body(x, False, False))
        body(rows - 1, False, True)

    @pl.when(p == 0)
    def _():
        def base(x, first, last):
            coeffs = stencil_coeffs(fib[x])
            for i in range(5):
                coef[i, x] = coeffs[i]
            gain = local_gain(reg[x], params)
            u = v[x]
            of_v, of_h, of_m, of_g, gate, push = reaction(u, h[x], gain)
            for i, value in enumerate((of_v, of_h, of_m, of_g)):
                gate_1[i, x] = value
            low = None if first else v[x - 1]
            high = None if last else v[x + 1]
            u_new = CENTRE * u + plane(u, low, high, coeffs) + DEPTH * depth_sum(u) + push - 0.1 * c[x]
            h_new = 0.75 * h[x] + 0.25 * gate
            for i, value in enumerate(reaction(u_new, h_new, gain)[:4]):
                gate_2[i, x] = value

        each_row(base)

    def step_1(x, first, last):
        u = tan[0, 0, x]
        coeffs = tuple(coef[i, x] for i in range(5))
        low = None if first else tan[0, 0, x - 1]
        high = None if last else tan[0, 0, x + 1]
        dv[x] = (
            gate_1[0, x] * u
            + plane(u, low, high, coeffs)
            + DEPTH * depth_sum(u)
            + gate_1[1, x] * tan[0, 1, x]
            + jnp.where(reg[x] == p, gate_1[2, x], 0.0)
            - 0.1 * tan[0, 2, x]
        )
        new_h = 0.75 * tan[0, 1, x] + gate_1[3, x] * u
        new_c = 0.96 * tan[0, 2, x] + 0.05 * u
        if first or last:
            out[0, 1, x] = new_h
            out[0, 2, x] = new_c
        else:
            dh[x] = new_h
            dc[x] = new_c

    each_row(step_1)
    out[0, 0, 0] = dv[0]
    out[0, 0, rows - 1] = dv[rows - 1]
    near[0, 0] = dv[1]
    near[1, 0] = dv[rows - 2]

    def step_2(x):
        u = dv[x]
        coeffs = tuple(coef[i, x] for i in range(5))
        out[0, 0, x] = (
            gate_2[0, x] * u
            + plane(u, dv[x - 1], dv[x + 1], coeffs)
            + DEPTH * depth_sum(u)
            + gate_2[1, x] * dh[x]
            + jnp.where(reg[x] == p, gate_2[2, x], 0.0)
            - 0.1 * dc[x]
        )
        out[0, 1, x] = 0.75 * dh[x] + gate_2[3, x] * u
        out[0, 2, x] = 0.96 * dc[x] + 0.05 * u

    pl.loop(1, rows - 1)(step_2)


def tail_kernel(params, v, h, c, reg, fib, tan, near, al, al_v, ar, ar_v, bl, bl_f, br, br_f, part, out, coef):
    side_at, step = pl.program_id(0), pl.program_id(1)
    chunk = part.shape[0]

    def run(side, edge, edge_v, beyond, beyond_f):
        outer, inner = (0, 1) if side == 0 else (1, 0)
        sign = -1 if side == 0 else 1

        def ordered(outside, inside):
            return (outside, inside) if side == 0 else (inside, outside)

        @pl.when(step == 0)
        def _():
            coeffs = stencil_coeffs(fib[outer])
            gain = local_gain(reg[outer], params)
            u = v[outer]
            _, _, _, _, gate, push = reaction(u, h[outer], gain)
            low, high = ordered(edge_v[0], v[inner])
            u_new = CENTRE * u + plane(u, low, high, coeffs) + DEPTH * depth_sum(u) + push - 0.1 * c[outer]
            h_new = 0.75 * h[outer] + 0.25 * gate
            of_v, of_h, of_m, of_g, _, _ = reaction(u_new, h_new, gain)
            next_x, _, _, next_b, next_a = stencil_coeffs(fib[inner])
            sent = beyond_f[0]
            there = sent > 0.5
            far_x, _, _, far_b, far_a = stencil_coeffs((sent - 1.0).astype(jnp.int32))
            values = coeffs + (of_v, of_h, of_m, of_g, next_x, next_b, next_a)
            values = values + (jnp.where(there, far_x, 0.0), jnp.where(there, far_b, 0.0), jnp.where(there, far_a, 0.0))
            for i, value in enumerate(values):
                coef[i] = value

        for j in range(chunk):
            p = step * chunk + j
            coeffs = tuple(coef[i] for i in range(5))
            extra = one_sided(edge[j], sign, coeffs[0], coeffs[3], coeffs[4])
            u = part[j, 0, outer] + extra
            outside = beyond[j] + one_sided(tan[j, 0, 0], -sign, coef[12], coef[13], coef[14])
            low, high = ordered(outside, near[0, j])
            dh, dc = part[j, 1, outer], part[j, 2, outer]
            out[j, 0, outer] = (
                coef[5] * u
                + plane(u, low, high, coeffs)
                + DEPTH * depth_sum(u)
                + coef[6] * dh
                + jnp.where(reg[outer] == p, coef[7], 0.0)
                - 0.1 * dc
            )
            out[j, 1, outer] = 0.75 * dh + coef[8] * u
            out[j, 2, outer] = 0.96 * dc + 0.05 * u
            out[j, 0, inner] = part[j, 0, inner] + one_sided(extra, sign, coef[9], coef[10], coef[11])
            out[j, 1, inner] = part[j, 1, inner]
            out[j, 2, inner] = part[j, 2, inner]

    pl.when(side_at == 0)(lambda: run(0, al, al_v, bl, bl_f))
    pl.when(side_at == 1)(lambda: run(1, ar, ar_v, br, br_f))


def gather_kernel(sites, dv, out):
    fields, _, _, levels, width = dv.shape
    lane = lax.broadcasted_iota(jnp.int32, (LANES, LANES), 1)

    @pl.loop(0, out.shape[0] // LANES)
    def _(block):
        def take(k, acc):
            site = sites[block * LANES + k]
            held = jnp.maximum(site, 0)
            x, y = held // width, held % width
            start = pl.multiple_of((y // LANES) * LANES, LANES)
            found = dv[:, 0, x, :, pl.ds(start, LANES)].reshape(LANES, LANES)
            turn = (k - y % LANES + LANES) % LANES
            return jnp.where(lane == jnp.where(site < 0, -1, k), pltpu.roll(found, turn, 1), acc)

        acc = lax.fori_loop(0, LANES, take, jnp.zeros((LANES, LANES), jnp.float32), unroll=4)
        out[pl.ds(pl.multiple_of(block * LANES, LANES), LANES), :] = acc.T


def compiler_params(mib):
    return pltpu.CompilerParams(vmem_limit_bytes=mib * MIB)


def shards(voltage, gating, recovery, tangents, parameters, region, fiber_class, electrode_site, electrode_owner):
    rows, levels, width = voltage.shape
    fields = tangents.shape[0]
    tiles = lax.axis_size("tx")
    f32 = jnp.float32
    up = [(i, i + 1) for i in range(tiles - 1)]
    down = [(i + 1, i) for i in range(tiles - 1)]
    smem = pl.BlockSpec(memory_space=pltpu.SMEM)
    hbm = pl.BlockSpec(memory_space=pl.ANY)
    row = (levels, width)
    sent = jax.ShapeDtypeStruct((fields + 1,) + row, f32)

    edge_low, edge_high = pl.pallas_call(
        edges_kernel,
        out_shape=(sent, sent),
        in_specs=[hbm, hbm],
        out_specs=(hbm, hbm),
        scratch_shapes=[pltpu.SemaphoreType.DMA((4,))],
        name="edges",
    )(tangents, voltage)
    from_right = lax.ppermute(edge_low, "tx", down)
    from_left = lax.ppermute(edge_high, "tx", up)

    chunk = 2
    pairs = rows // 2

    def at(index):
        return lambda *grid: index(*grid)

    side_specs, side_args = [], []
    for side in range(2):
        place = 0 if side == 0 else pairs - 1
        side_specs.append(pl.BlockSpec((chunk, 3, 2) + row, functools.partial(lambda q, i: (i, 0, q, 0, 0), place)))
        side_args.append(tangents)
        for array in (voltage, gating, region, fiber_class):
            side_specs.append(pl.BlockSpec((2,) + row, functools.partial(lambda q, i: (q, 0, 0), place)))
            side_args.append(array)
    whole_sent = pl.BlockSpec((fields + 1,) + row, lambda i: (0, 0, 0))
    part_low, part_high = pl.pallas_call(
        partial_kernel,
        grid=(fields // chunk,),
        out_shape=(sent, sent),
        in_specs=[smem] + side_specs,
        out_specs=(whole_sent, whole_sent),
        scratch_shapes=[pltpu.VMEM((2, 8) + row, f32)],
        compiler_params=compiler_params(24),
        name="partial",
    )(parameters, *side_args)
    beyond_right = lax.ppermute(part_low, "tx", down)
    beyond_left = lax.ppermute(part_high, "tx", up)

    owners = electrode_owner[:, 0]
    count = owners.shape[0]
    order = jnp.arange(count, dtype=jnp.int32)
    same = (owners[:, None] == owners[None, :]) & (order[:, None] < order[None, :])
    target = owners * CAP + jnp.sum(same.astype(jnp.int32), axis=0)
    slots = jnp.arange(tiles * CAP, dtype=jnp.int32)
    sites = jnp.max(jnp.where(target[:, None] == slots[None, :], electrode_site[:, None], -1), axis=0)

    field = pl.BlockSpec((rows,) + row, lambda p: (0, 0, 0))
    tan_spec = pl.BlockSpec((1, 3, rows) + row, lambda p: (p, 0, 0, 0, 0))
    tile = (rows,) + row
    partial_out, near = pl.pallas_call(
        main_kernel,
        grid=(fields,),
        out_shape=(jax.ShapeDtypeStruct(tangents.shape, f32), jax.ShapeDtypeStruct((2, fields) + row, f32)),
        in_specs=[smem] + [field] * 5 + [tan_spec],
        out_specs=(tan_spec, pl.BlockSpec((2, 1) + row, lambda p: (0, p, 0, 0))),
        scratch_shapes=[
            pltpu.VMEM((5,) + tile, f32),
            pltpu.VMEM((4,) + tile, f32),
            pltpu.VMEM((4,) + tile, f32),
            pltpu.VMEM(tile, f32),
            pltpu.VMEM(tile, f32),
            pltpu.VMEM(tile, f32),
        ],
        compiler_params=compiler_params(32),
        cost_estimate=pl.CostEstimate(flops=200_000_000, bytes_accessed=28 * MIB, transcendentals=300_000),
        name="interior",
    )(parameters, voltage, gating, recovery, region, fiber_class, tangents)

    ends = pairs - 1
    base = pl.BlockSpec((2,) + row, lambda s, i: (s * ends, 0, 0))
    left = pl.BlockSpec((chunk,) + row, lambda s, i: (i * (1 - s) + (fields // chunk - 1) * s, 0, 0))
    right = pl.BlockSpec((chunk,) + row, lambda s, i: (i * s, 0, 0))
    extra = pl.BlockSpec((1,) + row, lambda s, i: (fields, 0, 0))
    pair = pl.BlockSpec((chunk, 3, 2) + row, lambda s, i: (i, 0, s * ends, 0, 0))
    tangents_out = pl.pallas_call(
        tail_kernel,
        grid=(2, fields // chunk),
        out_shape=jax.ShapeDtypeStruct(tangents.shape, f32),
        in_specs=[smem]
        + [base] * 5
        + [
            pl.BlockSpec((chunk, 1, 1) + row, lambda s, i: (i, 0, s * (rows - 1), 0, 0)),
            pl.BlockSpec((1, chunk) + row, lambda s, i: (s, i, 0, 0)),
            left,
            extra,
            right,
            extra,
            left,
            extra,
            right,
            extra,
            pair,
        ],
        out_specs=pair,
        scratch_shapes=[pltpu.VMEM((15,) + row, f32)],
        input_output_aliases={16: 0},
        compiler_params=compiler_params(24),
        name="tail",
    )(
        parameters,
        voltage,
        gating,
        recovery,
        region,
        fiber_class,
        tangents,
        near,
        from_left,
        from_left,
        from_right,
        from_right,
        beyond_left,
        beyond_left,
        beyond_right,
        beyond_right,
        partial_out,
    )

    outgoing = pl.pallas_call(
        gather_kernel,
        grid=(1,),
        out_shape=jax.ShapeDtypeStruct((tiles * CAP, fields * levels), f32),
        in_specs=[smem, pl.BlockSpec((fields, 1, rows) + row, lambda i: (0, 0, 0, 0, 0))],
        out_specs=pl.BlockSpec((tiles * CAP, fields * levels), lambda i: (0, 0)),
        compiler_params=compiler_params(24),
        name="gather",
    )(sites, tangents_out)
    arrived = lax.all_to_all(
        outgoing.reshape(tiles, CAP, fields * levels), "tx", split_axis=0, concat_axis=0, tiled=True
    )
    return tangents_out, arrived.reshape(tiles * CAP, fields * levels)


def solution(mesh):
    line = P(("groups", "tx"), None, None)
    placed = (
        line,
        line,
        line,
        P(None, None, ("groups", "tx"), None, None),
        P("groups"),
        line,
        line,
        P(("groups", "tx")),
        P(("groups", "tx"), None),
    )
    return jax.shard_map(
        shards,
        mesh=mesh,
        in_specs=placed,
        out_specs=(P(None, None, ("groups", "tx"), None, None), P(("groups", "tx"), None)),
        check_vma=False,
    )
```

```python
import functools

import jax
import jax.numpy as jnp
from jax import lax
from jax.experimental import pallas as pl
from jax.experimental.pallas import tpu as pltpu
from jax.sharding import PartitionSpec as P

CAP = 16
GROUP = 8
LANES = 128
CHUNK = 2
MIB = 1 << 20

CENTRE = 0.7
DEPTH = 0.025


def rolled(x, shift, axis):
    return pltpu.roll(x, shift % x.shape[axis], axis)


def stencil_coeffs(fiber):
    width = fiber.shape[-1]
    x_coef = jnp.where(fiber == 0, 0.1, jnp.where(fiber == 2, 0.025, 0.0625))
    y_coef = 0.125 - x_coef
    w_coef = jnp.where(fiber == 1, 0.01875, jnp.where(fiber == 3, -0.01875, 0.0))
    return (x_coef,) + shifted_pair(y_coef, width) + shifted_pair(w_coef, width)


def shifted_pair(coef, width):
    lane = lax.broadcasted_iota(jnp.int32, coef.shape, 1)
    before = jnp.where(lane == 0, 0.0, rolled(coef, 1, 1))
    after = jnp.where(lane == width - 1, 0.0, rolled(coef, -1, 1))
    return before, after


def depth_sum(levels_of, k, count):
    u = levels_of(k)
    level = lax.broadcasted_iota(jnp.int32, u.shape, 0)
    first = u if k == 0 else rolled(levels_of(k - 1), 1, 0)
    last = u if k == count - 1 else rolled(levels_of(k + 1), -1, 0)
    return jnp.where(level == 0, first, rolled(u, 1, 0)) + jnp.where(level == GROUP - 1, last, rolled(u, -1, 0))


def plane(u, low, high, coeffs):
    x_coef, y_before, y_after, w_before, w_after = coeffs
    if low is None:
        total, gap = high, high
    elif high is None:
        total, gap = low, -low
    else:
        total, gap = low + high, high - low
    return (
        x_coef * total
        + rolled(y_before * u + w_before * gap, -1, 1)
        + rolled(y_after * u - w_after * gap, 1, 1)
    )


def one_sided(u, sign, x_coef, w_before, w_after):
    part = rolled(w_before * u, -1, 1) - rolled(w_after * u, 1, 1)
    return x_coef * u + part if sign > 0 else x_coef * u - part


def local_gain(region, params):
    gain = jnp.zeros(region.shape, jnp.float32)
    for p in range(params.shape[0]):
        gain = jnp.where(region == p, params[p], gain)
    return 0.2 * gain


def reaction(v, h, gain):
    current = v - v * v * v * (1.0 / 3.0)
    slope = 1.0 - v * v
    gate = 1.0 / (1.0 + jnp.exp(-4.0 * v))
    of_v = CENTRE + gain * h * slope
    return of_v, gain * current, 0.2 * h * current, gate * (1.0 - gate), gate, gain * h * current


def groups_of(levels):
    return [(k, pl.ds(GROUP * k, GROUP)) for k in range(levels // GROUP)]


def message_kernel(params, *refs):
    ins, (left, right), coef = refs[:10], refs[10:12], refs[12]
    chunk, fields = ins[0].shape[0], params.shape[0]
    groups = groups_of(ins[1].shape[1])
    step = pl.program_id(0)
    for side, out in ((0, left), (1, right)):
        tan, v, h, reg, fib = ins[5 * side : 5 * side + 5]
        outer, inner = (0, 1) if side == 0 else (1, 0)

        @pl.when(step == 0)
        def _():
            for _, z in groups:
                fiber = fib[outer, z]
                of_v, of_h, of_m, _, _, _ = reaction(v[outer, z], h[outer, z], local_gain(reg[outer, z], params))
                for i, value in enumerate(stencil_coeffs(fiber) + (of_v, of_h, of_m)):
                    coef[side, i, z] = value
                out[2 * fields, z] = v[outer, z]
                out[2 * fields + 1, z] = (fiber + 1).astype(jnp.float32)

        for j in range(chunk):
            p = step * chunk + j
            for k, z in groups:
                u, other = tan[j, 0, outer, z], tan[j, 0, inner, z]
                coeffs = tuple(coef[side, i, z] for i in range(5))
                low, high = (None, other) if side == 0 else (other, None)
                out[p, z] = u
                out[fields + p, z] = (
                    coef[side, 5, z] * u
                    + plane(u, low, high, coeffs)
                    + DEPTH * depth_sum(lambda i: tan[j, 0, outer, groups[i][1]], k, len(groups))
                    + coef[side, 6, z] * tan[j, 1, outer, z]
                    + jnp.where(reg[outer, z] == p, coef[side, 7, z], 0.0)
                    - 0.1 * tan[j, 2, outer, z]
                )


def main_kernel(params, v, h, c, reg, fib, tan, out, state, base_state, coef, gate_1, gate_2, dv, dh, dc):
    step = pl.program_id(0)
    rows, levels, _ = v.shape
    chunk = tan.shape[0]
    groups = groups_of(levels)

    def each_row(body):
        body(0, True, False)
        pl.loop(1, rows - 1)(lambda x: body(x, False, False))
        body(rows - 1, False, True)

    @pl.when(step == 0)
    def _():
        def base(x, first, last):
            for k, z in groups:
                coeffs = stencil_coeffs(fib[x, z])
                for i in range(5):
                    coef[i, x, z] = coeffs[i]
                gain = local_gain(reg[x, z], params)
                u = v[x, z]
                of_v, of_h, of_m, of_g, gate, push = reaction(u, h[x, z], gain)
                for i, value in enumerate((of_v, of_h, of_m, of_g)):
                    gate_1[i, x, z] = value
                low = None if first else v[x - 1, z]
                high = None if last else v[x + 1, z]
                depth = depth_sum(lambda i: v[x, groups[i][1]], k, len(groups))
                u_new = CENTRE * u + plane(u, low, high, coeffs) + DEPTH * depth + push - 0.1 * c[x, z]
                h_new = 0.75 * h[x, z] + 0.25 * gate
                if first or last:
                    values = coeffs + (u_new, h_new, gain, reg[x, z].astype(jnp.float32))
                    for i, value in enumerate(values):
                        base_state[int(last), i, z] = value
                else:
                    for i, value in enumerate(reaction(u_new, h_new, gain)[:4]):
                        gate_2[i, x, z] = value

        each_row(base)
        for side, x in ((0, 1), (1, rows - 2)):
            for i, at in enumerate((0, 3, 4)):
                base_state[side, 9 + i] = coef[at, x]

    def step_1(x, first, last):
        for k, z in groups:
            coeffs = tuple(coef[i, x, z] for i in range(5))
            for j in range(chunk):
                u = tan[j, 0, x, z]
                low = None if first else tan[j, 0, x - 1, z]
                high = None if last else tan[j, 0, x + 1, z]
                dv[j, x, z] = (
                    gate_1[0, x, z] * u
                    + plane(u, low, high, coeffs)
                    + DEPTH * depth_sum(lambda i: tan[j, 0, x, groups[i][1]], k, len(groups))
                    + gate_1[1, x, z] * tan[j, 1, x, z]
                    + jnp.where(reg[x, z] == step * chunk + j, gate_1[2, x, z], 0.0)
                    - 0.1 * tan[j, 2, x, z]
                )
                new_h = 0.75 * tan[j, 1, x, z] + gate_1[3, x, z] * u
                if first or last:
                    state[int(last), 0, j, z] = new_h
                    state[int(last), 1, j, z] = 0.096 * tan[j, 2, x, z] + 0.005 * u
                else:
                    dh[j, x, z] = new_h
                    dc[j, x, z] = 0.096 * tan[j, 2, x, z] + 0.005 * u

    each_row(step_1)

    def step_2(x):
        for k, z in groups:
            coeffs = tuple(coef[i, x, z] for i in range(5))
            for j in range(chunk):
                u = dv[j, x, z]
                out[j, 0, x, z] = (
                    gate_2[0, x, z] * u
                    + plane(u, dv[j, x - 1, z], dv[j, x + 1, z], coeffs)
                    + DEPTH * depth_sum(lambda i: dv[j, x, groups[i][1]], k, len(groups))
                    + gate_2[1, x, z] * dh[j, x, z]
                    + jnp.where(reg[x, z] == step * chunk + j, gate_2[2, x, z], 0.0)
                    - dc[j, x, z]
                )
                out[j, 1, x, z] = 0.75 * dh[j, x, z] + gate_2[3, x, z] * u
                out[j, 2, x, z] = 9.6 * dc[j, x, z] + 0.05 * u

    pl.loop(1, rows - 1)(step_2)
    for side, x in ((0, 1), (1, rows - 2)):
        for j in range(chunk):
            state[side, 2, j] = dv[j, x]
            state[side, 3, j] = out[j, 0, x]


def lay_columns(rows_of, laid, index):
    for at in range(laid.shape[1] // LANES):
        lanes = pl.ds(at * LANES, LANES)
        laid[index, lanes, :] = rows_of(lanes).reshape(LANES, LANES).T


def early_kernel(places, dv, out, laid):
    for at, x in enumerate(range(2, dv.shape[2] - 2)):
        lay_columns(lambda lanes: dv[:, 0, x, :, lanes], laid, at)
    width, count = laid.shape[1], laid.shape[0]
    flat = laid.reshape(count * width, laid.shape[2])

    def take(s, carry):
        place = places[s]
        out[pl.ds(s, 1), :] = jnp.where(place >= 0, flat[pl.ds(jnp.maximum(place, 0), 1), :], 0.0)
        return carry

    lax.fori_loop(0, out.shape[0], take, 0, unroll=8)


def tail_kernel(places, own_low, own_high, from_left, from_right, state, base_state, early, _, out, rows_out, dv, dh, dc, laid, coef, sems):
    fields, levels, width = dv.shape[2:]
    rows = out.shape[2]
    groups = groups_of(levels)
    copies = []
    for side, (own, there) in enumerate(((own_low, from_left), (own_high, from_right))):
        sign = -1 if side == 0 else 1

        def ordered(outside, inside):
            return (outside, inside) if side == 0 else (inside, outside)

        for k, z in groups:
            x_coef, y_before, y_after, w_before, w_after, v_new, h_new, gain = (base_state[side, i, z] for i in range(8))
            v_new = v_new + one_sided(there[2 * fields, z], sign, x_coef, w_before, w_after)
            for i, value in enumerate(reaction(v_new, h_new, gain)[:4]):
                coef[i, z] = value
            sent = there[2 * fields + 1, z]
            far = stencil_coeffs((sent - 1.0).astype(jnp.int32))
            for i, at in enumerate((0, 3, 4)):
                coef[4 + i, z] = jnp.where(sent > 0.5, far[at], 0.0)

        @pl.loop(0, fields)
        def _(p):
            for k, z in groups:
                x_coef, w_before, w_after = (base_state[side, i, z] for i in (0, 3, 4))
                extra = one_sided(there[p, z], sign, x_coef, w_before, w_after)
                dv[side, 0, p, z] = own[fields + p, z] + extra
                next_x, next_b, next_a = (base_state[side, 9 + i, z] for i in range(3))
                dv[side, 1, p, z] = state[side, 3, p, z] + one_sided(extra, sign, next_x, next_b, next_a)
            new = []
            for k, z in groups:
                u = dv[side, 0, p, z]
                outside = there[fields + p, z] + one_sided(own[p, z], -sign, coef[4, z], coef[5, z], coef[6, z])
                low, high = ordered(outside, state[side, 2, p, z])
                coeffs = tuple(base_state[side, i, z] for i in range(5))
                new.append(
                    coef[0, z] * u
                    + plane(u, low, high, coeffs)
                    + DEPTH * depth_sum(lambda i: dv[side, 0, p, groups[i][1]], k, len(groups))
                    + coef[1, z] * state[side, 0, p, z]
                    + jnp.where(base_state[side, 8, z] == p.astype(jnp.float32), coef[2, z], 0.0)
                    - state[side, 1, p, z]
                )
                dh[side, p, z] = 0.75 * state[side, 0, p, z] + coef[3, z] * u
                dc[side, p, z] = 9.6 * state[side, 1, p, z] + 0.05 * u
            for k, z in groups:
                dv[side, 0, p, z] = new[k]

        outer, inner = (0, 1) if side == 0 else (rows - 1, rows - 2)
        for i, (ref, target) in enumerate(
            (
                (dv.at[side, 0], out.at[:, 0, outer]),
                (dv.at[side, 1], out.at[:, 0, inner]),
                (dh.at[side], out.at[:, 1, outer]),
                (dc.at[side], out.at[:, 2, outer]),
            )
        ):
            copy = pltpu.make_async_copy(ref, target, sems.at[4 * side + i])
            copy.start()
            copies.append(copy)
        for i in range(2):
            lay_columns(lambda lanes: dv[side, i, :, :, lanes], laid, 2 * side + i)

    flat = laid.reshape(4 * width, laid.shape[2])

    def take(s, carry):
        place = places[s]
        line = pl.ds(s, 1)
        rows_out[line, :] = jnp.where(place >= 0, flat[pl.ds(jnp.maximum(place, 0), 1), :], early[line, :])
        return carry

    lax.fori_loop(0, rows_out.shape[0], take, 0, unroll=8)
    for copy in copies:
        copy.wait()


def compiler_params(mib):
    return pltpu.CompilerParams(vmem_limit_bytes=mib * MIB)


def shards(voltage, gating, recovery, tangents, parameters, region, fiber_class, electrode_site, electrode_owner):
    rows, levels, width = voltage.shape
    fields = tangents.shape[0]
    tiles = lax.axis_size("tx")
    f32 = jnp.float32
    up = [(i, i + 1) for i in range(tiles - 1)]
    down = [(i + 1, i) for i in range(tiles - 1)]
    smem = pl.BlockSpec(memory_space=pltpu.SMEM)
    hbm = pl.BlockSpec(memory_space=pl.ANY)
    vmem = pl.BlockSpec(memory_space=pltpu.VMEM)
    row = (levels, width)
    slots, depth = tiles * CAP, fields * levels
    message = jax.ShapeDtypeStruct((2 * fields + 2,) + row, f32)

    chunk = 2
    side_specs, side_args = [], []
    for side in range(2):
        place = 0 if side == 0 else rows // 2 - 1
        side_specs.append(pl.BlockSpec((chunk, 3, 2) + row, functools.partial(lambda q, i: (i, 0, q, 0, 0), place)))
        side_args.append(tangents)
        for array in (voltage, gating, region, fiber_class):
            side_specs.append(pl.BlockSpec((2,) + row, functools.partial(lambda q, i: (q, 0, 0), place)))
            side_args.append(array)
    whole = pl.BlockSpec(message.shape, lambda i: (0, 0, 0))
    own_low, own_high = pl.pallas_call(
        message_kernel,
        grid=(fields // chunk,),
        out_shape=(message, message),
        in_specs=[smem] + side_specs,
        out_specs=(whole, whole),
        scratch_shapes=[pltpu.VMEM((2, 8) + row, f32)],
        compiler_params=compiler_params(60),
        name="message",
    )(parameters, *side_args)
    from_right = lax.ppermute(own_low, "tx", down)
    from_left = lax.ppermute(own_high, "tx", up)

    owners = electrode_owner[:, 0]
    order = jnp.arange(owners.shape[0], dtype=jnp.int32)
    same = (owners[:, None] == owners[None, :]) & (order[:, None] < order[None, :])
    target = owners * CAP + jnp.sum(same.astype(jnp.int32), axis=0)
    sites = jnp.max(
        jnp.where(target[:, None] == jnp.arange(slots, dtype=jnp.int32)[None, :], electrode_site[:, None], -1), axis=0
    )
    site_x, site_y = sites // width, sites % width
    inside = (site_x >= 2) & (site_x < rows - 2) & (sites >= 0)
    early_places = jnp.where(inside, sites - 2 * width, -1)
    edge_row = jnp.where(site_x < 2, site_x, 2 + (rows - 1 - site_x))
    late_places = jnp.where(inside | (sites < 0), -1, edge_row * width + site_y)

    field = pl.BlockSpec((rows,) + row, lambda i: (0, 0, 0))
    tan_spec = pl.BlockSpec((CHUNK, 3, rows) + row, lambda i: (i, 0, 0, 0, 0))
    tile = (rows,) + row
    partial_out, state, base_state = pl.pallas_call(
        main_kernel,
        grid=(fields // CHUNK,),
        out_shape=(
            jax.ShapeDtypeStruct(tangents.shape, f32),
            jax.ShapeDtypeStruct((2, 4, fields) + row, f32),
            jax.ShapeDtypeStruct((2, 12) + row, f32),
        ),
        in_specs=[smem] + [field] * 5 + [tan_spec],
        out_specs=(
            tan_spec,
            pl.BlockSpec((2, 4, CHUNK) + row, lambda i: (0, 0, i, 0, 0)),
            pl.BlockSpec((2, 12) + row, lambda i: (0, 0, 0, 0)),
        ),
        scratch_shapes=[
            pltpu.VMEM((5,) + tile, f32),
            pltpu.VMEM((4,) + tile, f32),
            pltpu.VMEM((4,) + tile, f32),
            pltpu.VMEM((CHUNK,) + tile, f32),
            pltpu.VMEM((CHUNK,) + tile, f32),
            pltpu.VMEM((CHUNK,) + tile, f32),
        ],
        compiler_params=compiler_params(56),
        cost_estimate=pl.CostEstimate(flops=200_000_000, bytes_accessed=28 * MIB, transcendentals=300_000),
        name="interior",
    )(parameters, voltage, gating, recovery, region, fiber_class, tangents)

    early = pl.pallas_call(
        early_kernel,
        grid=(1,),
        out_shape=jax.ShapeDtypeStruct((slots, depth), f32),
        in_specs=[smem, pl.BlockSpec((fields, 1, rows) + row, lambda i: (0, 0, 0, 0, 0))],
        out_specs=pl.BlockSpec((slots, depth), lambda i: (0, 0)),
        scratch_shapes=[pltpu.VMEM((rows - 4, width, depth), f32)],
        compiler_params=compiler_params(56),
        cost_estimate=pl.CostEstimate(flops=20_000_000, bytes_accessed=12 * MIB, transcendentals=0),
        name="early",
    )(early_places, partial_out)

    tangents_out, outgoing = pl.pallas_call(
        tail_kernel,
        out_shape=(jax.ShapeDtypeStruct(tangents.shape, f32), jax.ShapeDtypeStruct((slots, depth), f32)),
        in_specs=[smem] + [vmem] * 7 + [hbm],
        out_specs=(hbm, vmem),
        scratch_shapes=[
            pltpu.VMEM((2, 2, fields) + row, f32),
            pltpu.VMEM((2, fields) + row, f32),
            pltpu.VMEM((2, fields) + row, f32),
            pltpu.VMEM((4, width, depth), f32),
            pltpu.VMEM((7,) + row, f32),
            pltpu.SemaphoreType.DMA((8,)),
        ],
        input_output_aliases={8: 0},
        compiler_params=compiler_params(32),
        name="tail",
    )(late_places, own_low, own_high, from_left, from_right, state, base_state, early, partial_out)

    arrived = lax.all_to_all(outgoing.reshape(tiles, CAP, depth), "tx", split_axis=0, concat_axis=0, tiled=True)
    return tangents_out, arrived.reshape(slots, depth)


def solution(mesh):
    line = P(("groups", "tx"), None, None)
    placed = (
        line,
        line,
        line,
        P(None, None, ("groups", "tx"), None, None),
        P("groups"),
        line,
        line,
        P(("groups", "tx")),
        P(("groups", "tx"), None),
    )
    return jax.shard_map(
        shards,
        mesh=mesh,
        in_specs=placed,
        out_specs=(P(None, None, ("groups", "tx"), None, None), P(("groups", "tx"), None)),
        check_vma=False,
    )
```

```python
import functools

import jax
import jax.numpy as jnp
from jax import lax
from jax.experimental import pallas as pl
from jax.experimental.pallas import tpu as pltpu
from jax.sharding import PartitionSpec as P

CAP = 16
GROUP = 8
LANES = 128
CHUNK = 2
MESSAGE_MIB = 54
MIB = 1 << 20

CENTRE = 0.7
DEPTH = 0.025


def rolled(x, shift, axis):
    return pltpu.roll(x, shift % x.shape[axis], axis)


def stencil_coeffs(fiber):
    width = fiber.shape[-1]
    x_coef = jnp.where(fiber == 0, 0.1, jnp.where(fiber == 2, 0.025, 0.0625))
    y_coef = 0.125 - x_coef
    w_coef = jnp.where(fiber == 1, 0.01875, jnp.where(fiber == 3, -0.01875, 0.0))
    return (x_coef,) + shifted_pair(y_coef, width) + shifted_pair(w_coef, width)


def shifted_pair(coef, width):
    lane = lax.broadcasted_iota(jnp.int32, coef.shape, 1)
    before = jnp.where(lane == 0, 0.0, rolled(coef, 1, 1))
    after = jnp.where(lane == width - 1, 0.0, rolled(coef, -1, 1))
    return before, after


def depth_sum(levels_of, k, count):
    u = levels_of(k)
    level = lax.broadcasted_iota(jnp.int32, u.shape, 0)
    first = u if k == 0 else rolled(levels_of(k - 1), 1, 0)
    last = u if k == count - 1 else rolled(levels_of(k + 1), -1, 0)
    return jnp.where(level == 0, first, rolled(u, 1, 0)) + jnp.where(level == GROUP - 1, last, rolled(u, -1, 0))


def plane(u, outside, inside, coeffs):
    x_coef, y_before, y_after, w_before, w_after = coeffs
    if outside is None:
        total, gap = inside, -inside
    else:
        total, gap = outside + inside, outside - inside
    return (
        x_coef * total
        + rolled(y_before * u + w_before * gap, -1, 1)
        + rolled(y_after * u - w_after * gap, 1, 1)
    )


def one_sided(u, x_coef, w_before, w_after):
    return x_coef * u + rolled(w_before * u, -1, 1) - rolled(w_after * u, 1, 1)


def signed(coeffs, sign):
    x_coef, y_before, y_after, w_before, w_after = coeffs
    return x_coef, y_before, y_after, sign * w_before, sign * w_after


def local_gain(region, params):
    gain = jnp.zeros(region.shape, jnp.float32)
    for p in range(params.shape[0]):
        gain = jnp.where(region == p, params[p], gain)
    return 0.2 * gain


def reaction(v, h, gain):
    current = v - v * v * v * (1.0 / 3.0)
    slope = 1.0 - v * v
    gate = 1.0 / (1.0 + jnp.exp(-4.0 * v))
    of_v = CENTRE + gain * h * slope
    return of_v, gain * current, 0.2 * h * current, gate * (1.0 - gate), gate, gain * h * current


def groups_of(levels):
    return [(k, pl.ds(GROUP * k, GROUP)) for k in range(levels // GROUP)]


def edge_of(side, rows):
    return side * (rows - 1), 1 + side * (rows - 3), (2 * side - 1).astype(jnp.float32)


def message_kernel(side_at, params, tan, v, h, reg, fib, out, dv, dhc, base, label, coef, sems):
    fields, rows = tan.shape[0], tan.shape[2]
    groups = groups_of(tan.shape[3])
    outer, inner, sign = edge_of(side_at[0], rows)
    half = fields // 2
    pairs = [
        (v.at[outer], out.at[2 * fields]),
        (h.at[outer], base),
        (reg.at[outer], label.at[0]),
        (fib.at[outer], label.at[1]),
    ]
    for at in (0, half):
        part = pl.ds(at, half)
        pairs += [
            (tan.at[part, 0, outer], out.at[part]),
            (tan.at[part, 0, inner], dv.at[part]),
            (tan.at[part, 1, outer], dhc.at[0, part]),
            (tan.at[part, 2, outer], dhc.at[1, part]),
        ]
    copies = [pltpu.make_async_copy(a, b, sems.at[k]) for k, (a, b) in enumerate(pairs)]
    for copy in copies:
        copy.start()

    for copy in copies[:4]:
        copy.wait()
    for _, z in groups:
        fiber = label[1, z]
        gain = local_gain(label[0, z], params)
        of_v, of_h, of_m, _, _, _ = reaction(out[2 * fields, z], base[z], gain)
        for i, value in enumerate(signed(stencil_coeffs(fiber), sign) + (of_v, of_h, of_m)):
            coef[i, z] = value
        out[2 * fields + 1, z] = (fiber + 1).astype(jnp.float32)

    for at in range(2):
        for copy in copies[4 + 4 * at : 8 + 4 * at]:
            copy.wait()

        @pl.loop(at * half // CHUNK, (at + 1) * half // CHUNK)
        def _(step):
            for k, z in groups:
                coeffs = tuple(coef[i, z] for i in range(5))
                for j in range(CHUNK):
                    p = step * CHUNK + j
                    u = out[p, z]
                    out[fields + p, z] = (
                        coef[5, z] * u
                        + plane(u, None, dv[p, z], coeffs)
                        + DEPTH * depth_sum(lambda i: out[p, groups[i][1]], k, len(groups))
                        + coef[6, z] * dhc[0, p, z]
                        + jnp.where(label[0, z] == p, coef[7, z], 0.0)
                        - 0.1 * dhc[1, p, z]
                    )


def main_kernel(
    side_at, params, v, h, c, reg, fib, tan, edge, out, state, base_state, held, now, later, rest,
    coef, gate_1, gate_2, dv, dh, dc
):
    step = pl.program_id(0)
    rows, levels, _ = v.shape
    link_outer, _, _ = edge_of(1 - side_at[0], rows)
    chip_outer, chip_inner, _ = edge_of(side_at[0], rows)
    chunk = tan.shape[0]
    groups = groups_of(levels)
    ends = ((0, 0), (1, rows - 1))

    @pl.when(step == 0)
    def _():
        def base(x, low, high, side):
            for k, z in groups:
                coeffs = stencil_coeffs(fib[x, z])
                gain = local_gain(reg[x, z], params)
                u = v[x, z]
                of_v, of_h, of_m, of_g, gate, push = reaction(u, h[x, z], gain)
                if side is not None:
                    coeffs = signed(coeffs, 2.0 * side - 1.0)
                for i in range(5):
                    coef[i, x, z] = coeffs[i]
                for i, value in enumerate((of_v, of_h, of_m, of_g)):
                    gate_1[i, x, z] = value
                depth = depth_sum(lambda i: v[x, groups[i][1]], k, len(groups))
                around = plane(u, v[high, z] if side is None else None, v[low, z], coeffs)
                u_new = CENTRE * u + around + DEPTH * depth + push - 0.1 * c[x, z]
                h_new = 0.75 * h[x, z] + 0.25 * gate
                if side is None:
                    for i, value in enumerate(reaction(u_new, h_new, gain)[:4]):
                        gate_2[i, x, z] = value
                else:
                    values = coeffs + (u_new, h_new, gain, reg[x, z].astype(jnp.float32))
                    for i, value in enumerate(values):
                        base_state[side, i, z] = value

        pl.loop(1, rows - 1)(lambda x: base(x, x - 1, x + 1, None))
        base(0, 1, None, 0)
        base(rows - 1, rows - 2, None, 1)
        for side, x in ((0, 1), (1, rows - 2)):
            base_state[side, 9] = coef[0, x]
            base_state[side, 10] = (2.0 * side - 1.0) * coef[3, x]
            base_state[side, 11] = (2.0 * side - 1.0) * coef[4, x]
        rest[0] = v[chip_outer]
        rest[1] = (fib[chip_outer] + 1).astype(jnp.float32)

    for j in range(chunk):
        dv[j, link_outer] = edge[j]
    for k, z in groups:
        coeffs = tuple(coef[i, chip_outer, z] for i in range(5))
        for j in range(chunk):
            u = tan[j, 0, chip_outer, z]
            new = (
                gate_1[0, chip_outer, z] * u
                + plane(u, None, tan[j, 0, chip_inner, z], coeffs)
                + DEPTH * depth_sum(lambda i: tan[j, 0, chip_outer, groups[i][1]], k, len(groups))
                + gate_1[1, chip_outer, z] * tan[j, 1, chip_outer, z]
                + jnp.where(reg[chip_outer, z] == step * chunk + j, gate_1[2, chip_outer, z], 0.0)
                - 0.1 * tan[j, 2, chip_outer, z]
            )
            dv[j, chip_outer, z] = new
            now[j, z] = u
            later[j, z] = new
    for side, x in ends:
        for k, z in groups:
            for j in range(chunk):
                u = tan[j, 0, x, z]
                state[side, 0, j, z] = 0.75 * tan[j, 1, x, z] + gate_1[3, x, z] * u
                state[side, 1, j, z] = 0.096 * tan[j, 2, x, z] + 0.005 * u

    def step_1(x):
        for k, z in groups:
            coeffs = tuple(coef[i, x, z] for i in range(5))
            for j in range(chunk):
                u = tan[j, 0, x, z]
                dv[j, x, z] = (
                    gate_1[0, x, z] * u
                    + plane(u, tan[j, 0, x + 1, z], tan[j, 0, x - 1, z], coeffs)
                    + DEPTH * depth_sum(lambda i: tan[j, 0, x, groups[i][1]], k, len(groups))
                    + gate_1[1, x, z] * tan[j, 1, x, z]
                    + jnp.where(reg[x, z] == step * chunk + j, gate_1[2, x, z], 0.0)
                    - 0.1 * tan[j, 2, x, z]
                )
                dh[j, x, z] = 0.75 * tan[j, 1, x, z] + gate_1[3, x, z] * u
                dc[j, x, z] = 0.096 * tan[j, 2, x, z] + 0.005 * u

    pl.loop(1, rows - 1)(step_1)

    def step_2(x):
        for k, z in groups:
            coeffs = tuple(coef[i, x, z] for i in range(5))
            for j in range(chunk):
                u = dv[j, x, z]
                new = (
                    gate_2[0, x, z] * u
                    + plane(u, dv[j, x + 1, z], dv[j, x - 1, z], coeffs)
                    + DEPTH * depth_sum(lambda i: dv[j, x, groups[i][1]], k, len(groups))
                    + gate_2[1, x, z] * dh[j, x, z]
                    + jnp.where(reg[x, z] == step * chunk + j, gate_2[2, x, z], 0.0)
                    - dc[j, x, z]
                )
                out[j, 0, x, z] = new
                held[j, x - 1, z] = new
                out[j, 1, x, z] = 0.75 * dh[j, x, z] + gate_2[3, x, z] * u
                out[j, 2, x, z] = 9.6 * dc[j, x, z] + 0.05 * u

    pl.loop(1, rows - 1)(step_2)
    for side, x in ((0, 1), (1, rows - 2)):
        for j in range(chunk):
            state[side, 2, j] = dv[j, x]


def lay_columns(rows_of, laid, index):
    for at in range(laid.shape[1] // LANES):
        lanes = pl.ds(at * LANES, LANES)
        laid[index, lanes, :] = rows_of(lanes).reshape(LANES, LANES).T


def take_columns(sites, laid, out, first, other):
    count, width, depth = laid.shape
    flat = laid.reshape(count * width, depth)

    def take(s, carry):
        place = sites[s] - first * width
        here = (sites[s] >= 0) & (place >= 0) & (place < count * width)
        line = pl.ds(s, 1)
        out[line, :] = jnp.where(here, flat[pl.ds(jnp.where(here, place, 0), 1), :], other(line))
        return carry

    lax.fori_loop(0, out.shape[0], take, 0, unroll=8)


def tail_kernel(side_at, sites, state, base_state, held, _, *refs):
    out, lines, dv, dh, dc, laid, coef, sems = refs[-8:]
    fields, levels, width = dv.shape[1:]
    if len(refs) == 11:
        own, there, before = refs[:3]
        now, later = own.at[pl.ds(0, fields)], own.at[pl.ds(fields, fields)]
        far_now, far_later, far_rest = (there.at[pl.ds(i * fields, fields if i < 2 else 2)] for i in range(3))
    else:
        now, later, far_now, far_later, far_rest = refs[:5]
        before = None
    rows = out.shape[2]
    groups = groups_of(levels)
    side = side_at[0]
    outer, inner, sign = edge_of(side, rows)

    for _, z in groups:
        v_new = base_state[side, 5, z] + one_sided(far_rest[0, z], *(base_state[side, i, z] for i in (0, 3, 4)))
        for i, value in enumerate(reaction(v_new, base_state[side, 6, z], base_state[side, 7, z])[:4]):
            coef[i, z] = value
        sent = far_rest[1, z]
        far = signed(stencil_coeffs((sent - 1.0).astype(jnp.int32)), -sign)
        for i, at in enumerate((0, 3, 4)):
            coef[4 + i, z] = jnp.where(sent > 0.5, far[at], 0.0)

    @pl.loop(0, fields // CHUNK)
    def _(step):
        for k, z in groups:
            own_row = tuple(base_state[side, i, z] for i in (0, 3, 4))
            next_row = tuple(base_state[side, 9 + i, z] for i in range(3))
            for j in range(CHUNK):
                p = step * CHUNK + j
                extra = one_sided(far_now[p, z], *own_row)
                dv[0, p, z] = later[p, z] + extra
                dv[1, p, z] = held[p, inner - 1, z] + one_sided(extra, *next_row)
        for k, z in groups:
            coeffs = tuple(base_state[side, i, z] for i in range(5))
            far = tuple(coef[i, z] for i in (4, 5, 6))
            for j in range(CHUNK):
                p = step * CHUNK + j
                u = dv[0, p, z]
                outside = far_later[p, z] + one_sided(now[p, z], *far)
                dv[2, p, z] = (
                    coef[0, z] * u
                    + plane(u, outside, state[side, 2, p, z], coeffs)
                    + DEPTH * depth_sum(lambda i: dv[0, p, groups[i][1]], k, len(groups))
                    + coef[1, z] * state[side, 0, p, z]
                    + jnp.where(base_state[side, 8, z] == p.astype(jnp.float32), coef[2, z], 0.0)
                    - state[side, 1, p, z]
                )
                dh[p, z] = 0.75 * state[side, 0, p, z] + coef[3, z] * u
                dc[p, z] = 9.6 * state[side, 1, p, z] + 0.05 * u

    copies = [
        pltpu.make_async_copy(ref, target, sems.at[i])
        for i, (ref, target) in enumerate(
            (
                (dv.at[2], out.at[:, 0, outer]),
                (dv.at[1], out.at[:, 0, inner]),
                (dh, out.at[:, 1, outer]),
                (dc, out.at[:, 2, outer]),
            )
        )
    ]
    for copy in copies:
        copy.start()
    count = laid.shape[0]
    first = side * (rows - count)
    lay_columns(lambda lanes: dv[2, :, :, lanes], laid, outer - first)
    lay_columns(lambda lanes: dv[1, :, :, lanes], laid, inner - first)
    if before is None:
        for x in range(2, rows - 2):
            lay_columns(lambda lanes: held[:, x - 1, :, lanes], laid, x - first)
    take_columns(
        sites, laid, lines, first, lambda line: jnp.zeros_like(lines[line, :]) if before is None else before[line, :]
    )
    for copy in copies:
        copy.wait()


def compiler_params(mib):
    return pltpu.CompilerParams(vmem_limit_bytes=mib * MIB)


def swapped(message, first, tiles):
    pairs = [(i, i + 1) for i in range(first, tiles - 1, 2)]
    return lax.ppermute(message, "tx", pairs + [(b, a) for a, b in pairs])


def shards(voltage, gating, recovery, tangents, parameters, region, fiber_class, electrode_site, electrode_owner):
    rows, levels, width = voltage.shape
    fields = tangents.shape[0]
    tiles = lax.axis_size("tx")
    f32 = jnp.float32
    smem = pl.BlockSpec(memory_space=pltpu.SMEM)
    hbm = pl.BlockSpec(memory_space=pl.ANY)
    vmem = pl.BlockSpec(memory_space=pltpu.VMEM)
    row = (levels, width)
    slots, depth = tiles * CAP, fields * levels
    linked = (lax.axis_index("tx") % 2).astype(jnp.int32)
    link_side, chip_side = linked.reshape(1), (1 - linked).reshape(1)

    message = jax.ShapeDtypeStruct((2 * fields + 2,) + row, f32)
    over_link = pl.pallas_call(
        message_kernel,
        out_shape=message,
        in_specs=[smem, smem] + [hbm] * 5,
        out_specs=vmem,
        scratch_shapes=[
            pltpu.VMEM((fields,) + row, f32),
            pltpu.VMEM((2, fields) + row, f32),
            pltpu.VMEM(row, f32),
            pltpu.VMEM((2,) + row, jnp.int32),
            pltpu.VMEM((8,) + row, f32),
            pltpu.SemaphoreType.DMA((12,)),
        ],
        compiler_params=compiler_params(MESSAGE_MIB),
        cost_estimate=pl.CostEstimate(flops=1_000_000_000, bytes_accessed=MIB, transcendentals=0),
        name="message",
    )(link_side, parameters, tangents, voltage, gating, region, fiber_class)
    from_link = swapped(over_link, 1, tiles)

    owners = electrode_owner[:, 0]
    order = jnp.arange(owners.shape[0], dtype=jnp.int32)
    same = (owners[:, None] == owners[None, :]) & (order[:, None] < order[None, :])
    target = owners * CAP + jnp.sum(same.astype(jnp.int32), axis=0)
    sites = jnp.max(
        jnp.where(target[:, None] == jnp.arange(slots, dtype=jnp.int32)[None, :], electrode_site[:, None], -1), axis=0
    )

    field = pl.BlockSpec((rows,) + row, lambda i: (0, 0, 0))
    tan_spec = pl.BlockSpec((CHUNK, 3, rows) + row, lambda i: (i, 0, 0, 0, 0))
    edge_spec = pl.BlockSpec((CHUNK,) + row, lambda i: (fields // CHUNK + i, 0, 0))
    tile = (rows,) + row
    partial_out, state, base_state, held, now, later, rest = pl.pallas_call(
        main_kernel,
        grid=(fields // CHUNK,),
        out_shape=(
            jax.ShapeDtypeStruct(tangents.shape, f32),
            jax.ShapeDtypeStruct((2, 3, fields) + row, f32),
            jax.ShapeDtypeStruct((2, 12) + row, f32),
            jax.ShapeDtypeStruct((fields, rows - 2) + row, f32),
            jax.ShapeDtypeStruct((fields,) + row, f32),
            jax.ShapeDtypeStruct((fields,) + row, f32),
            jax.ShapeDtypeStruct((2,) + row, f32),
        ),
        in_specs=[smem, smem] + [field] * 5 + [tan_spec, edge_spec],
        out_specs=(
            tan_spec,
            pl.BlockSpec((2, 3, CHUNK) + row, lambda i: (0, 0, i, 0, 0)),
            pl.BlockSpec((2, 12) + row, lambda i: (0, 0, 0, 0)),
            pl.BlockSpec((CHUNK, rows - 2) + row, lambda i: (i, 0, 0, 0)),
            pl.BlockSpec((CHUNK,) + row, lambda i: (i, 0, 0)),
            pl.BlockSpec((CHUNK,) + row, lambda i: (i, 0, 0)),
            pl.BlockSpec((2,) + row, lambda i: (0, 0, 0)),
        ),
        scratch_shapes=[
            pltpu.VMEM((5,) + tile, f32),
            pltpu.VMEM((4,) + tile, f32),
            pltpu.VMEM((4,) + tile, f32),
            pltpu.VMEM((CHUNK,) + tile, f32),
            pltpu.VMEM((CHUNK,) + tile, f32),
            pltpu.VMEM((CHUNK,) + tile, f32),
        ],
        compiler_params=compiler_params(36),
        cost_estimate=pl.CostEstimate(flops=1000, bytes_accessed=1024, transcendentals=0),
        name="interior",
    )(chip_side, parameters, voltage, gating, recovery, region, fiber_class, tangents, over_link)
    from_chip = tuple(swapped(part, 0, tiles) for part in (now, later, rest))

    def tail(side_at, filled, *messages):
        return pl.pallas_call(
            tail_kernel,
            out_shape=(jax.ShapeDtypeStruct(tangents.shape, f32), jax.ShapeDtypeStruct((slots, depth), f32)),
            in_specs=[smem, smem] + [vmem] * 3 + [hbm] + [vmem] * len(messages),
            out_specs=(hbm, vmem),
            scratch_shapes=[
                pltpu.VMEM((3, fields) + row, f32),
                pltpu.VMEM((fields,) + row, f32),
                pltpu.VMEM((fields,) + row, f32),
                pltpu.VMEM((2 if len(messages) == 3 else rows - 2, width, depth), f32),
                pltpu.VMEM((7,) + row, f32),
                pltpu.SemaphoreType.DMA((4,)),
            ],
            input_output_aliases={5: 0},
            compiler_params=compiler_params(20),
            cost_estimate=pl.CostEstimate(flops=1000, bytes_accessed=1024, transcendentals=0),
            name="tail",
        )(side_at, sites, state, base_state, held, filled, *messages)

    filled, lines = tail(chip_side, partial_out, now, later, *from_chip)
    from_link, lines = lax.optimization_barrier((from_link, lines))
    tangents_out, outgoing = tail(link_side, filled, over_link, from_link, lines)

    arrived = lax.all_to_all(outgoing.reshape(tiles, CAP, depth), "tx", split_axis=0, concat_axis=0, tiled=True)
    return tangents_out, arrived.reshape(slots, depth)


def solution(mesh):
    line = P(("groups", "tx"), None, None)
    placed = (
        line,
        line,
        line,
        P(None, None, ("groups", "tx"), None, None),
        P("groups"),
        line,
        line,
        P(("groups", "tx")),
        P(("groups", "tx"), None),
    )
    return jax.shard_map(
        shards,
        mesh=mesh,
        in_specs=placed,
        out_specs=(P(None, None, ("groups", "tx"), None, None), P(("groups", "tx"), None)),
        check_vma=False,
    )
```

```python
import functools

import jax
import jax.numpy as jnp
from jax import lax
from jax.experimental import pallas as pl
from jax.experimental.pallas import tpu as pltpu
from jax.sharding import PartitionSpec as P

CAP = 16
GROUP = 8
LANES = 128
CHUNK = 2
MESSAGE_MIB = 54
INTERIOR_MIB = 36
MIB = 1 << 20

CENTRE = 0.7
DEPTH = 0.025


def rolled(x, shift, axis):
    return pltpu.roll(x, shift % x.shape[axis], axis)


def stencil_coeffs(fiber):
    width = fiber.shape[-1]
    x_coef = jnp.where(fiber == 0, 0.1, jnp.where(fiber == 2, 0.025, 0.0625))
    y_coef = 0.125 - x_coef
    w_coef = jnp.where(fiber == 1, 0.01875, jnp.where(fiber == 3, -0.01875, 0.0))
    return (x_coef,) + shifted_pair(y_coef, width) + shifted_pair(w_coef, width)


def shifted_pair(coef, width):
    lane = lax.broadcasted_iota(jnp.int32, coef.shape, 1)
    before = jnp.where(lane == 0, 0.0, rolled(coef, 1, 1))
    after = jnp.where(lane == width - 1, 0.0, rolled(coef, -1, 1))
    return before, after


def depth_sum(levels_of, k, count):
    u = levels_of(k)
    level = lax.broadcasted_iota(jnp.int32, u.shape, 0)
    first = u if k == 0 else rolled(levels_of(k - 1), 1, 0)
    last = u if k == count - 1 else rolled(levels_of(k + 1), -1, 0)
    return jnp.where(level == 0, first, rolled(u, 1, 0)) + jnp.where(level == GROUP - 1, last, rolled(u, -1, 0))


def plane(u, outside, inside, coeffs):
    x_coef, y_before, y_after, w_before, w_after = coeffs
    if outside is None:
        total, gap = inside, -inside
    else:
        total, gap = outside + inside, outside - inside
    return (
        x_coef * total
        + rolled(y_before * u + w_before * gap, -1, 1)
        + rolled(y_after * u - w_after * gap, 1, 1)
    )


def one_sided(u, x_coef, w_before, w_after):
    return x_coef * u + rolled(w_before * u, -1, 1) - rolled(w_after * u, 1, 1)


def signed(coeffs, sign):
    x_coef, y_before, y_after, w_before, w_after = coeffs
    return x_coef, y_before, y_after, sign * w_before, sign * w_after


def local_gain(region, params):
    gain = jnp.zeros(region.shape, jnp.float32)
    for p in range(params.shape[0]):
        gain = jnp.where(region == p, params[p], gain)
    return 0.2 * gain


def reaction(v, h, gain):
    current = v - v * v * v * (1.0 / 3.0)
    slope = 1.0 - v * v
    gate = 1.0 / (1.0 + jnp.exp(-4.0 * v))
    of_v = CENTRE + gain * h * slope
    return of_v, gain * current, 0.2 * h * current, gate * (1.0 - gate), gate, gain * h * current


def groups_of(levels):
    return [(k, pl.ds(GROUP * k, GROUP)) for k in range(levels // GROUP)]


def edge_of(side, rows):
    return side * (rows - 1), 1 + side * (rows - 3), (2 * side - 1).astype(jnp.float32)


def message_kernel(side_at, params, tan, v, h, reg, fib, sent, out, dv, dhc, base, label, coef, sems, sent_sems):
    fields, rows = tan.shape[0], tan.shape[2]
    groups = groups_of(tan.shape[3])
    outer, inner, sign = edge_of(side_at[0], rows)
    half = fields // 2
    pairs = [
        (v.at[outer], out.at[2 * fields]),
        (h.at[outer], base),
        (reg.at[outer], label.at[0]),
        (fib.at[outer], label.at[1]),
    ]
    for at in (0, half):
        part = pl.ds(at, half)
        pairs += [
            (tan.at[part, 0, outer], out.at[part]),
            (tan.at[part, 0, inner], dv.at[part]),
            (tan.at[part, 1, outer], dhc.at[0, part]),
            (tan.at[part, 2, outer], dhc.at[1, part]),
        ]
    copies = [pltpu.make_async_copy(a, b, sems.at[k]) for k, (a, b) in enumerate(pairs)]
    for copy in copies:
        copy.start()

    def send(first, count, k):
        part = pl.ds(first, count)
        return pltpu.make_async_copy(out.at[part], sent.at[part], sent_sems.at[k])

    for copy in copies[:4]:
        copy.wait()
    for _, z in groups:
        fiber = label[1, z]
        gain = local_gain(label[0, z], params)
        of_v, of_h, of_m, _, _, _ = reaction(out[2 * fields, z], base[z], gain)
        for i, value in enumerate(signed(stencil_coeffs(fiber), sign) + (of_v, of_h, of_m)):
            coef[i, z] = value
        out[2 * fields + 1, z] = (fiber + 1).astype(jnp.float32)
    send(2 * fields, 2, 0).start()

    for at in range(2):
        for copy in copies[4 + 4 * at : 8 + 4 * at]:
            copy.wait()
        send(at * half, half, 1 + at).start()

        @pl.loop(at * half // CHUNK, (at + 1) * half // CHUNK)
        def _(step):
            for k, z in groups:
                coeffs = tuple(coef[i, z] for i in range(5))
                for j in range(CHUNK):
                    p = step * CHUNK + j
                    u = out[p, z]
                    out[fields + p, z] = (
                        coef[5, z] * u
                        + plane(u, None, dv[p, z], coeffs)
                        + DEPTH * depth_sum(lambda i: out[p, groups[i][1]], k, len(groups))
                        + coef[6, z] * dhc[0, p, z]
                        + jnp.where(label[0, z] == p, coef[7, z], 0.0)
                        - 0.1 * dhc[1, p, z]
                    )
            send(fields + step * CHUNK, CHUNK, 3).start()

    send(2 * fields, 2, 0).wait()
    for at in range(2):
        send(at * half, half, 1 + at).wait()
    send(fields, fields, 3).wait()


def main_kernel(
    side_at, params, v, h, c, reg, fib, tan_all, out, state, base_state, held, now, later, rest,
    coef, gate_1, gate_2, dv, dh, dc, slots, sems
):
    step = pl.program_id(0)
    rows, levels, _ = v.shape
    chip_outer, _, _ = edge_of(side_at[0], rows)
    chunk, count = CHUNK, pl.num_programs(0)
    groups = groups_of(levels)
    ends = ((0, 0), (1, rows - 1))
    tan = slots.at[step % 2]

    def load(at, slot):
        return pltpu.make_async_copy(tan_all.at[pl.ds(at * chunk, chunk)], slots.at[slot], sems.at[slot])

    @pl.when(step == 0)
    def _():
        for slot in range(2):
            load(slot, slot).start()

    @pl.when(step == 0)
    def _():
        def base(x, low, high, side):
            for k, z in groups:
                coeffs = stencil_coeffs(fib[x, z])
                gain = local_gain(reg[x, z], params)
                u = v[x, z]
                of_v, of_h, of_m, of_g, gate, push = reaction(u, h[x, z], gain)
                if side is not None:
                    coeffs = signed(coeffs, 2.0 * side - 1.0)
                for i in range(5):
                    coef[i, x, z] = coeffs[i]
                for i, value in enumerate((of_v, of_h, of_m, of_g)):
                    gate_1[i, x, z] = value
                depth = depth_sum(lambda i: v[x, groups[i][1]], k, len(groups))
                around = plane(u, v[high, z] if side is None else None, v[low, z], coeffs)
                u_new = CENTRE * u + around + DEPTH * depth + push - 0.1 * c[x, z]
                h_new = 0.75 * h[x, z] + 0.25 * gate
                if side is None:
                    for i, value in enumerate(reaction(u_new, h_new, gain)[:4]):
                        gate_2[i, x, z] = value
                else:
                    values = coeffs + (u_new, h_new, gain, reg[x, z].astype(jnp.float32))
                    for i, value in enumerate(values):
                        base_state[side, i, z] = value

        pl.loop(1, rows - 1)(lambda x: base(x, x - 1, x + 1, None))
        base(0, 1, None, 0)
        base(rows - 1, rows - 2, None, 1)
        for side, x in ((0, 1), (1, rows - 2)):
            base_state[side, 9] = coef[0, x]
            base_state[side, 10] = (2.0 * side - 1.0) * coef[3, x]
            base_state[side, 11] = (2.0 * side - 1.0) * coef[4, x]
        rest[0] = v[chip_outer]
        rest[1] = (fib[chip_outer] + 1).astype(jnp.float32)

    load(step, step % 2).wait()
    for side, x in ends:
        inside = 1 if side == 0 else rows - 2
        for k, z in groups:
            coeffs = tuple(coef[i, x, z] for i in range(5))
            for j in range(chunk):
                u = tan[j, 0, x, z]
                dv[j, x, z] = (
                    gate_1[0, x, z] * u
                    + plane(u, None, tan[j, 0, inside, z], coeffs)
                    + DEPTH * depth_sum(lambda i: tan[j, 0, x, groups[i][1]], k, len(groups))
                    + gate_1[1, x, z] * tan[j, 1, x, z]
                    + jnp.where(reg[x, z] == step * chunk + j, gate_1[2, x, z], 0.0)
                    - 0.1 * tan[j, 2, x, z]
                )
                state[side, 0, j, z] = 0.75 * tan[j, 1, x, z] + gate_1[3, x, z] * u
                state[side, 1, j, z] = 0.096 * tan[j, 2, x, z] + 0.005 * u
    for j in range(chunk):
        now[j] = tan[j, 0, chip_outer]
        later[j] = dv[j, chip_outer]

    def step_1(x):
        for k, z in groups:
            coeffs = tuple(coef[i, x, z] for i in range(5))
            for j in range(chunk):
                u = tan[j, 0, x, z]
                dv[j, x, z] = (
                    gate_1[0, x, z] * u
                    + plane(u, tan[j, 0, x + 1, z], tan[j, 0, x - 1, z], coeffs)
                    + DEPTH * depth_sum(lambda i: tan[j, 0, x, groups[i][1]], k, len(groups))
                    + gate_1[1, x, z] * tan[j, 1, x, z]
                    + jnp.where(reg[x, z] == step * chunk + j, gate_1[2, x, z], 0.0)
                    - 0.1 * tan[j, 2, x, z]
                )
                dh[j, x, z] = 0.75 * tan[j, 1, x, z] + gate_1[3, x, z] * u
                dc[j, x, z] = 0.096 * tan[j, 2, x, z] + 0.005 * u

    pl.loop(1, rows - 1)(step_1)

    @pl.when(step + 2 < count)
    def _():
        load(step + 2, step % 2).start()

    def step_2(x):
        for k, z in groups:
            coeffs = tuple(coef[i, x, z] for i in range(5))
            for j in range(chunk):
                u = dv[j, x, z]
                new = (
                    gate_2[0, x, z] * u
                    + plane(u, dv[j, x + 1, z], dv[j, x - 1, z], coeffs)
                    + DEPTH * depth_sum(lambda i: dv[j, x, groups[i][1]], k, len(groups))
                    + gate_2[1, x, z] * dh[j, x, z]
                    + jnp.where(reg[x, z] == step * chunk + j, gate_2[2, x, z], 0.0)
                    - dc[j, x, z]
                )
                out[j, 0, x, z] = new
                held[j, x - 1, z] = new
                out[j, 1, x, z] = 0.75 * dh[j, x, z] + gate_2[3, x, z] * u
                out[j, 2, x, z] = 9.6 * dc[j, x, z] + 0.05 * u

    pl.loop(1, rows - 1)(step_2)
    for side, x in ((0, 1), (1, rows - 2)):
        for j in range(chunk):
            state[side, 2, j] = dv[j, x]


def lay_columns(rows_of, laid, index):
    for at in range(laid.shape[1] // LANES):
        lanes = pl.ds(at * LANES, LANES)
        laid[index, lanes, :] = rows_of(lanes).reshape(LANES, LANES).T


def take_columns(sites, laid, out, first, other):
    count, width, depth = laid.shape
    flat = laid.reshape(count * width, depth)

    def take(s, carry):
        place = sites[s] - first * width
        here = (sites[s] >= 0) & (place >= 0) & (place < count * width)
        line = pl.ds(s, 1)
        out[line, :] = jnp.where(here, flat[pl.ds(jnp.where(here, place, 0), 1), :], other(line))
        return carry

    lax.fori_loop(0, out.shape[0], take, 0, unroll=8)


def tail_kernel(side_at, sites, state, base_state, held, _, *refs):
    out, lines, dv, dh, dc, laid, coef, sems = refs[-8:]
    fields, levels, width = dv.shape[1:]
    if len(refs) == 11:
        own, there, before = refs[:3]
        now, later = own.at[pl.ds(0, fields)], own.at[pl.ds(fields, fields)]
        far_now, far_later, far_rest = (there.at[pl.ds(i * fields, fields if i < 2 else 2)] for i in range(3))
    else:
        now, later, far_now, far_later, far_rest = refs[:5]
        before = None
    rows = out.shape[2]
    groups = groups_of(levels)
    side = side_at[0]
    outer, inner, sign = edge_of(side, rows)

    for _, z in groups:
        v_new = base_state[side, 5, z] + one_sided(far_rest[0, z], *(base_state[side, i, z] for i in (0, 3, 4)))
        for i, value in enumerate(reaction(v_new, base_state[side, 6, z], base_state[side, 7, z])[:4]):
            coef[i, z] = value
        sent = far_rest[1, z]
        far = signed(stencil_coeffs((sent - 1.0).astype(jnp.int32)), -sign)
        for i, at in enumerate((0, 3, 4)):
            coef[4 + i, z] = jnp.where(sent > 0.5, far[at], 0.0)

    def stores(part):
        pairs = ((dv.at[2], 0, outer), (dv.at[1], 0, inner), (dh, 1, outer), (dc, 2, outer))
        return [pltpu.make_async_copy(a.at[part], out.at[part, f, x], sems.at[i]) for i, (a, f, x) in enumerate(pairs)]

    @pl.loop(0, fields // CHUNK)
    def _(step):
        for k, z in groups:
            own_row = tuple(base_state[side, i, z] for i in (0, 3, 4))
            next_row = tuple(base_state[side, 9 + i, z] for i in range(3))
            for j in range(CHUNK):
                p = step * CHUNK + j
                extra = one_sided(far_now[p, z], *own_row)
                dv[0, p, z] = later[p, z] + extra
                dv[1, p, z] = held[p, inner - 1, z] + one_sided(extra, *next_row)
        for k, z in groups:
            coeffs = tuple(base_state[side, i, z] for i in range(5))
            far = tuple(coef[i, z] for i in (4, 5, 6))
            for j in range(CHUNK):
                p = step * CHUNK + j
                u = dv[0, p, z]
                outside = far_later[p, z] + one_sided(now[p, z], *far)
                dv[2, p, z] = (
                    coef[0, z] * u
                    + plane(u, outside, state[side, 2, p, z], coeffs)
                    + DEPTH * depth_sum(lambda i: dv[0, p, groups[i][1]], k, len(groups))
                    + coef[1, z] * state[side, 0, p, z]
                    + jnp.where(base_state[side, 8, z] == p.astype(jnp.float32), coef[2, z], 0.0)
                    - state[side, 1, p, z]
                )
                dh[p, z] = 0.75 * state[side, 0, p, z] + coef[3, z] * u
                dc[p, z] = 9.6 * state[side, 1, p, z] + 0.05 * u

        for copy in stores(pl.ds(step * CHUNK, CHUNK)):
            copy.start()

    count = laid.shape[0]
    first = side * (rows - count)
    lay_columns(lambda lanes: dv[2, :, :, lanes], laid, outer - first)
    lay_columns(lambda lanes: dv[1, :, :, lanes], laid, inner - first)
    if before is None:
        for x in range(2, rows - 2):
            lay_columns(lambda lanes: held[:, x - 1, :, lanes], laid, x - first)
    take_columns(
        sites, laid, lines, first, lambda line: jnp.zeros_like(lines[line, :]) if before is None else before[line, :]
    )
    for copy in stores(pl.ds(0, fields)):
        copy.wait()


def compiler_params(mib):
    return pltpu.CompilerParams(vmem_limit_bytes=mib * MIB)


def swapped(message, first, tiles):
    pairs = [(i, i + 1) for i in range(first, tiles - 1, 2)]
    return lax.ppermute(message, "tx", pairs + [(b, a) for a, b in pairs])


def shards(voltage, gating, recovery, tangents, parameters, region, fiber_class, electrode_site, electrode_owner):
    rows, levels, width = voltage.shape
    fields = tangents.shape[0]
    tiles = lax.axis_size("tx")
    f32 = jnp.float32
    smem = pl.BlockSpec(memory_space=pltpu.SMEM)
    hbm = pl.BlockSpec(memory_space=pl.ANY)
    vmem = pl.BlockSpec(memory_space=pltpu.VMEM)
    row = (levels, width)
    slots, depth = tiles * CAP, fields * levels
    linked = (lax.axis_index("tx") % 2).astype(jnp.int32)
    link_side, chip_side = linked.reshape(1), (1 - linked).reshape(1)

    message = jax.ShapeDtypeStruct((2 * fields + 2,) + row, f32)
    over_link = pl.pallas_call(
        message_kernel,
        out_shape=message,
        in_specs=[smem, smem] + [hbm] * 5,
        out_specs=hbm,
        scratch_shapes=[
            pltpu.VMEM(message.shape, f32),
            pltpu.VMEM((fields,) + row, f32),
            pltpu.VMEM((2, fields) + row, f32),
            pltpu.VMEM(row, f32),
            pltpu.VMEM((2,) + row, jnp.int32),
            pltpu.VMEM((8,) + row, f32),
            pltpu.SemaphoreType.DMA((12,)),
            pltpu.SemaphoreType.DMA((4,)),
        ],
        compiler_params=compiler_params(MESSAGE_MIB),
        cost_estimate=pl.CostEstimate(flops=1_000_000_000, bytes_accessed=MIB, transcendentals=0),
        name="message",
    )(link_side, parameters, tangents, voltage, gating, region, fiber_class)
    from_link = swapped(over_link, 1, tiles)

    owners = electrode_owner[:, 0]
    order = jnp.arange(owners.shape[0], dtype=jnp.int32)
    same = (owners[:, None] == owners[None, :]) & (order[:, None] < order[None, :])
    target = owners * CAP + jnp.sum(same.astype(jnp.int32), axis=0)
    sites = jnp.max(
        jnp.where(target[:, None] == jnp.arange(slots, dtype=jnp.int32)[None, :], electrode_site[:, None], -1), axis=0
    )

    field = pl.BlockSpec((rows,) + row, lambda i: (0, 0, 0))
    tan_spec = pl.BlockSpec((CHUNK, 3, rows) + row, lambda i: (i, 0, 0, 0, 0))
    tile = (rows,) + row
    partial_out, state, base_state, held, now, later, rest = pl.pallas_call(
        main_kernel,
        grid=(fields // CHUNK,),
        out_shape=(
            jax.ShapeDtypeStruct(tangents.shape, f32),
            jax.ShapeDtypeStruct((2, 3, fields) + row, f32),
            jax.ShapeDtypeStruct((2, 12) + row, f32),
            jax.ShapeDtypeStruct((fields, rows - 2) + row, f32),
            jax.ShapeDtypeStruct((fields,) + row, f32),
            jax.ShapeDtypeStruct((fields,) + row, f32),
            jax.ShapeDtypeStruct((2,) + row, f32),
        ),
        in_specs=[smem, smem] + [field] * 5 + [hbm],
        out_specs=(
            tan_spec,
            pl.BlockSpec((2, 3, CHUNK) + row, lambda i: (0, 0, i, 0, 0)),
            pl.BlockSpec((2, 12) + row, lambda i: (0, 0, 0, 0)),
            pl.BlockSpec((CHUNK, rows - 2) + row, lambda i: (i, 0, 0, 0)),
            pl.BlockSpec((CHUNK,) + row, lambda i: (i, 0, 0)),
            pl.BlockSpec((CHUNK,) + row, lambda i: (i, 0, 0)),
            pl.BlockSpec((2,) + row, lambda i: (0, 0, 0)),
        ),
        scratch_shapes=[
            pltpu.VMEM((5,) + tile, f32),
            pltpu.VMEM((4,) + tile, f32),
            pltpu.VMEM((4,) + tile, f32),
            pltpu.VMEM((CHUNK,) + tile, f32),
            pltpu.VMEM((CHUNK,) + tile, f32),
            pltpu.VMEM((CHUNK,) + tile, f32),
            pltpu.VMEM((2, CHUNK, 3, rows) + row, f32),
            pltpu.SemaphoreType.DMA((2,)),
        ],
        compiler_params=compiler_params(INTERIOR_MIB),
        cost_estimate=pl.CostEstimate(flops=1000, bytes_accessed=1024, transcendentals=0),
        name="interior",
    )(chip_side, parameters, voltage, gating, recovery, region, fiber_class, tangents)
    from_chip = tuple(swapped(part, 0, tiles) for part in (now, later, rest))

    def tail(side_at, filled, *messages):
        return pl.pallas_call(
            tail_kernel,
            out_shape=(jax.ShapeDtypeStruct(tangents.shape, f32), jax.ShapeDtypeStruct((slots, depth), f32)),
            in_specs=[smem, smem] + [vmem] * 3 + [hbm] + [vmem] * len(messages),
            out_specs=(hbm, vmem),
            scratch_shapes=[
                pltpu.VMEM((3, fields) + row, f32),
                pltpu.VMEM((fields,) + row, f32),
                pltpu.VMEM((fields,) + row, f32),
                pltpu.VMEM((2 if len(messages) == 3 else rows - 2, width, depth), f32),
                pltpu.VMEM((7,) + row, f32),
                pltpu.SemaphoreType.DMA((4,)),
            ],
            input_output_aliases={5: 0},
            compiler_params=compiler_params(20),
            cost_estimate=pl.CostEstimate(flops=1000, bytes_accessed=1024, transcendentals=0),
            name="tail",
        )(side_at, sites, state, base_state, held, filled, *messages)

    filled, lines = tail(chip_side, partial_out, now, later, *from_chip)
    from_link, lines = lax.optimization_barrier((from_link, lines))
    tangents_out, outgoing = tail(link_side, filled, over_link, from_link, lines)

    arrived = lax.all_to_all(outgoing.reshape(tiles, CAP, depth), "tx", split_axis=0, concat_axis=0, tiled=True)
    return tangents_out, arrived.reshape(slots, depth)


def solution(mesh):
    line = P(("groups", "tx"), None, None)
    placed = (
        line,
        line,
        line,
        P(None, None, ("groups", "tx"), None, None),
        P("groups"),
        line,
        line,
        P(("groups", "tx")),
        P(("groups", "tx"), None),
    )
    return jax.shard_map(
        shards,
        mesh=mesh,
        in_specs=placed,
        out_specs=(P(None, None, ("groups", "tx"), None, None), P(("groups", "tx"), None)),
        check_vma=False,
    )
```

```python
import functools

import jax
import jax.numpy as jnp
from jax import lax
from jax.experimental import pallas as pl
from jax.experimental.pallas import tpu as pltpu
from jax.sharding import PartitionSpec as P

CAP = 16
GROUP = 8
LANES = 128
CHUNK = 2
WIDE = 1
MESSAGE_MIB = 54
INTERIOR_MIB = 36
MIB = 1 << 20

CENTRE = 0.7
DEPTH = 0.025


def rolled(x, shift, axis):
    return pltpu.roll(x, shift % x.shape[axis], axis)


def stencil_coeffs(fiber):
    width = fiber.shape[-1]
    x_coef = jnp.where(fiber == 0, 0.1, jnp.where(fiber == 2, 0.025, 0.0625))
    y_coef = 0.125 - x_coef
    w_coef = jnp.where(fiber == 1, 0.01875, jnp.where(fiber == 3, -0.01875, 0.0))
    return (x_coef,) + shifted_pair(y_coef, width) + shifted_pair(w_coef, width)


def shifted_pair(coef, width):
    lane = lax.broadcasted_iota(jnp.int32, coef.shape, 1)
    before = jnp.where(lane == 0, 0.0, rolled(coef, 1, 1))
    after = jnp.where(lane == width - 1, 0.0, rolled(coef, -1, 1))
    return before, after


def depth_sum(levels_of, k, count):
    u = levels_of(k)
    level = lax.broadcasted_iota(jnp.int32, u.shape, 0)
    first = u if k == 0 else rolled(levels_of(k - 1), 1, 0)
    last = u if k == count - 1 else rolled(levels_of(k + 1), -1, 0)
    return jnp.where(level == 0, first, rolled(u, 1, 0)) + jnp.where(level == GROUP - 1, last, rolled(u, -1, 0))


def plane(u, outside, inside, coeffs):
    x_coef, y_before, y_after, w_before, w_after = coeffs
    if outside is None:
        total, gap = inside, -inside
    else:
        total, gap = outside + inside, outside - inside
    return (
        x_coef * total
        + rolled(y_before * u + w_before * gap, -1, 1)
        + rolled(y_after * u - w_after * gap, 1, 1)
    )


def one_sided(u, x_coef, w_before, w_after):
    return x_coef * u + rolled(w_before * u, -1, 1) - rolled(w_after * u, 1, 1)


def signed(coeffs, sign):
    x_coef, y_before, y_after, w_before, w_after = coeffs
    return x_coef, y_before, y_after, sign * w_before, sign * w_after


def local_gain(region, params):
    gain = jnp.zeros(region.shape, jnp.float32)
    for p in range(params.shape[0]):
        gain = jnp.where(region == p, params[p], gain)
    return 0.2 * gain


def reaction(v, h, gain):
    current = v - v * v * v * (1.0 / 3.0)
    slope = 1.0 - v * v
    gate = 1.0 / (1.0 + jnp.exp(-4.0 * v))
    of_v = CENTRE + gain * h * slope
    return of_v, gain * current, 0.2 * h * current, gate * (1.0 - gate), gate, gain * h * current


def groups_of(levels):
    return [(k, pl.ds(GROUP * k, GROUP)) for k in range(levels // GROUP)]


def edge_of(side, rows):
    return side * (rows - 1), 1 + side * (rows - 3), (2 * side - 1).astype(jnp.float32)


def message_kernel(side_at, params, tan, v, h, reg, fib, sent, out, dv, dhc, base, label, coef, sems, sent_sems):
    fields, rows = tan.shape[0], tan.shape[2]
    groups = groups_of(tan.shape[3])
    outer, inner, sign = edge_of(side_at[0], rows)
    half = fields // 2
    pairs = [
        (v.at[outer], out.at[2 * fields]),
        (h.at[outer], base),
        (reg.at[outer], label.at[0]),
        (fib.at[outer], label.at[1]),
    ]
    for at in (0, half):
        part = pl.ds(at, half)
        pairs += [
            (tan.at[part, 0, outer], out.at[part]),
            (tan.at[part, 0, inner], dv.at[part]),
            (tan.at[part, 1, outer], dhc.at[0, part]),
            (tan.at[part, 2, outer], dhc.at[1, part]),
        ]
    copies = [pltpu.make_async_copy(a, b, sems.at[k]) for k, (a, b) in enumerate(pairs)]
    for copy in copies:
        copy.start()

    def send(first, count, k):
        part = pl.ds(first, count)
        return pltpu.make_async_copy(out.at[part], sent.at[part], sent_sems.at[k])

    for copy in copies[:4]:
        copy.wait()
    for _, z in groups:
        fiber = label[1, z]
        gain = local_gain(label[0, z], params)
        of_v, of_h, of_m, _, _, _ = reaction(out[2 * fields, z], base[z], gain)
        for i, value in enumerate(signed(stencil_coeffs(fiber), sign) + (of_v, of_h, of_m)):
            coef[i, z] = value
        out[2 * fields + 1, z] = (fiber + 1).astype(jnp.float32)
    send(2 * fields, 2, 0).start()

    for at in range(2):
        for copy in copies[4 + 4 * at : 8 + 4 * at]:
            copy.wait()
        send(at * half, half, 1 + at).start()

        @pl.loop(at * half // CHUNK, (at + 1) * half // CHUNK)
        def _(step):
            for k, z in groups:
                coeffs = tuple(coef[i, z] for i in range(5))
                for j in range(CHUNK):
                    p = step * CHUNK + j
                    u = out[p, z]
                    out[fields + p, z] = (
                        coef[5, z] * u
                        + plane(u, None, dv[p, z], coeffs)
                        + DEPTH * depth_sum(lambda i: out[p, groups[i][1]], k, len(groups))
                        + coef[6, z] * dhc[0, p, z]
                        + jnp.where(label[0, z] == p, coef[7, z], 0.0)
                        - 0.1 * dhc[1, p, z]
                    )
            send(fields + step * CHUNK, CHUNK, 3).start()

    send(2 * fields, 2, 0).wait()
    for at in range(2):
        send(at * half, half, 1 + at).wait()
    send(fields, fields, 3).wait()


def main_kernel(
    side_at, params, v, h, c, reg, fib, tan_all, out, state, base_state, held, now, later, rest,
    coef, gate_1, gate_2, dv, dh, dc, slots, sems
):
    step = pl.program_id(0)
    rows, levels, _ = v.shape
    chip_outer, _, _ = edge_of(side_at[0], rows)
    chunk, count = CHUNK, pl.num_programs(0)
    groups = groups_of(levels)
    ends = ((0, 0), (1, rows - 1))
    tan = slots.at[step % 2]

    def load(at, slot):
        return pltpu.make_async_copy(tan_all.at[pl.ds(at * chunk, chunk)], slots.at[slot], sems.at[slot])

    @pl.when(step == 0)
    def _():
        for slot in range(2):
            load(slot, slot).start()

    @pl.when(step == 0)
    def _():
        def base(x, low, high, side):
            for k, z in groups:
                coeffs = stencil_coeffs(fib[x, z])
                gain = local_gain(reg[x, z], params)
                u = v[x, z]
                of_v, of_h, of_m, of_g, gate, push = reaction(u, h[x, z], gain)
                if side is not None:
                    coeffs = signed(coeffs, 2.0 * side - 1.0)
                for i in range(5):
                    coef[i, x, z] = coeffs[i]
                for i, value in enumerate((of_v, of_h, of_m, of_g)):
                    gate_1[i, x, z] = value
                depth = depth_sum(lambda i: v[x, groups[i][1]], k, len(groups))
                around = plane(u, v[high, z] if side is None else None, v[low, z], coeffs)
                u_new = CENTRE * u + around + DEPTH * depth + push - 0.1 * c[x, z]
                h_new = 0.75 * h[x, z] + 0.25 * gate
                if side is None:
                    for i, value in enumerate(reaction(u_new, h_new, gain)[:4]):
                        gate_2[i, x, z] = value
                else:
                    values = coeffs + (u_new, h_new, gain, reg[x, z].astype(jnp.float32))
                    for i, value in enumerate(values):
                        base_state[side, i, z] = value

        pl.loop(1, rows - 1)(lambda x: base(x, x - 1, x + 1, None))
        base(0, 1, None, 0)
        base(rows - 1, rows - 2, None, 1)
        for side, x in ((0, 1), (1, rows - 2)):
            base_state[side, 9] = coef[0, x]
            base_state[side, 10] = (2.0 * side - 1.0) * coef[3, x]
            base_state[side, 11] = (2.0 * side - 1.0) * coef[4, x]
        rest[0] = v[chip_outer]
        rest[1] = (fib[chip_outer] + 1).astype(jnp.float32)

    load(step, step % 2).wait()
    for side, x in ends:
        inside = 1 if side == 0 else rows - 2
        for k, z in groups:
            coeffs = tuple(coef[i, x, z] for i in range(5))
            for j in range(chunk):
                u = tan[j, 0, x, z]
                dv[j, x, z] = (
                    gate_1[0, x, z] * u
                    + plane(u, None, tan[j, 0, inside, z], coeffs)
                    + DEPTH * depth_sum(lambda i: tan[j, 0, x, groups[i][1]], k, len(groups))
                    + gate_1[1, x, z] * tan[j, 1, x, z]
                    + jnp.where(reg[x, z] == step * chunk + j, gate_1[2, x, z], 0.0)
                    - 0.1 * tan[j, 2, x, z]
                )
                state[side, 0, j, z] = 0.75 * tan[j, 1, x, z] + gate_1[3, x, z] * u
                state[side, 1, j, z] = 0.096 * tan[j, 2, x, z] + 0.005 * u
    for j in range(chunk):
        now[j] = tan[j, 0, chip_outer]
        later[j] = dv[j, chip_outer]

    def step_1(x):
        for k, z in groups:
            coeffs = tuple(coef[i, x, z] for i in range(5))
            for j in range(chunk):
                u = tan[j, 0, x, z]
                dv[j, x, z] = (
                    gate_1[0, x, z] * u
                    + plane(u, tan[j, 0, x + 1, z], tan[j, 0, x - 1, z], coeffs)
                    + DEPTH * depth_sum(lambda i: tan[j, 0, x, groups[i][1]], k, len(groups))
                    + gate_1[1, x, z] * tan[j, 1, x, z]
                    + jnp.where(reg[x, z] == step * chunk + j, gate_1[2, x, z], 0.0)
                    - 0.1 * tan[j, 2, x, z]
                )
                dh[j, x, z] = 0.75 * tan[j, 1, x, z] + gate_1[3, x, z] * u
                dc[j, x, z] = 0.096 * tan[j, 2, x, z] + 0.005 * u

    pl.loop(1, rows - 1)(step_1)

    @pl.when(step + 2 < count)
    def _():
        load(step + 2, step % 2).start()

    def step_2(x):
        for k, z in groups:
            coeffs = tuple(coef[i, x, z] for i in range(5))
            for j in range(chunk):
                u = dv[j, x, z]
                new = (
                    gate_2[0, x, z] * u
                    + plane(u, dv[j, x + 1, z], dv[j, x - 1, z], coeffs)
                    + DEPTH * depth_sum(lambda i: dv[j, x, groups[i][1]], k, len(groups))
                    + gate_2[1, x, z] * dh[j, x, z]
                    + jnp.where(reg[x, z] == step * chunk + j, gate_2[2, x, z], 0.0)
                    - dc[j, x, z]
                )
                out[j, 0, x, z] = new
                held[j, x - 1, z] = new
                out[j, 1, x, z] = 0.75 * dh[j, x, z] + gate_2[3, x, z] * u
                out[j, 2, x, z] = 9.6 * dc[j, x, z] + 0.05 * u

    pl.loop(1, rows - 1)(step_2)
    for side, x in ((0, 1), (1, rows - 2)):
        for j in range(chunk):
            state[side, 2, j] = dv[j, x]


def lay_columns(rows_of, laid, index):
    for at in range(laid.shape[1] // LANES):
        lanes = pl.ds(at * LANES, LANES)
        laid[index, lanes, :] = rows_of(lanes).reshape(LANES, LANES).T


def take_columns(sites, laid, out, first, other):
    count, width, depth = laid.shape
    flat = laid.reshape(count * width, depth)

    def take(s, carry):
        place = sites[s] - first * width
        here = (sites[s] >= 0) & (place >= 0) & (place < count * width)
        line = pl.ds(s, 1)
        out[line, :] = jnp.where(here, flat[pl.ds(jnp.where(here, place, 0), 1), :], other(line))
        return carry

    lax.fori_loop(0, out.shape[0], take, 0, unroll=8)


def tail_kernel(side_at, sites, state, base_state, held, _, *refs):
    out, lines, dv, dh, dc, laid, coef, sems = refs[-8:]
    fields, levels, width = dv.shape[1:]
    if len(refs) == 11:
        own, there, before = refs[:3]
        now, later = own.at[pl.ds(0, fields)], own.at[pl.ds(fields, fields)]
        far_now, far_later, far_rest = (there.at[pl.ds(i * fields, fields if i < 2 else 2)] for i in range(3))
    else:
        now, later, far_now, far_later, far_rest = refs[:5]
        before = None
    rows = out.shape[2]
    groups = groups_of(levels)
    side = side_at[0]
    outer, inner, sign = edge_of(side, rows)

    for _, z in groups:
        v_new = base_state[side, 5, z] + one_sided(far_rest[0, z], *(base_state[side, i, z] for i in (0, 3, 4)))
        for i, value in enumerate(reaction(v_new, base_state[side, 6, z], base_state[side, 7, z])[:4]):
            coef[i, z] = value
        sent = far_rest[1, z]
        far = signed(stencil_coeffs((sent - 1.0).astype(jnp.int32)), -sign)
        for i, at in enumerate((0, 3, 4)):
            coef[4 + i, z] = jnp.where(sent > 0.5, far[at], 0.0)

    def stores(part):
        pairs = ((dv.at[2], 0, outer), (dv.at[1], 0, inner), (dh, 1, outer), (dc, 2, outer))
        return [pltpu.make_async_copy(a.at[part], out.at[part, f, x], sems.at[i]) for i, (a, f, x) in enumerate(pairs)]

    @pl.loop(0, fields // WIDE)
    def _(step):
        for k, z in groups:
            own_row = tuple(base_state[side, i, z] for i in (0, 3, 4))
            next_row = tuple(base_state[side, 9 + i, z] for i in range(3))
            for j in range(WIDE):
                p = step * WIDE + j
                extra = one_sided(far_now[p, z], *own_row)
                dv[0, p, z] = later[p, z] + extra
                dv[1, p, z] = held[p, inner - 1, z] + one_sided(extra, *next_row)
        for k, z in groups:
            coeffs = tuple(base_state[side, i, z] for i in range(5))
            far = tuple(coef[i, z] for i in (4, 5, 6))
            for j in range(WIDE):
                p = step * WIDE + j
                u = dv[0, p, z]
                outside = far_later[p, z] + one_sided(now[p, z], *far)
                dv[2, p, z] = (
                    coef[0, z] * u
                    + plane(u, outside, state[side, 2, p, z], coeffs)
                    + DEPTH * depth_sum(lambda i: dv[0, p, groups[i][1]], k, len(groups))
                    + coef[1, z] * state[side, 0, p, z]
                    + jnp.where(base_state[side, 8, z] == p.astype(jnp.float32), coef[2, z], 0.0)
                    - state[side, 1, p, z]
                )
                dh[p, z] = 0.75 * state[side, 0, p, z] + coef[3, z] * u
                dc[p, z] = 9.6 * state[side, 1, p, z] + 0.05 * u

        for copy in stores(pl.ds(step * WIDE, WIDE)):
            copy.start()

    count = laid.shape[0]
    first = side * (rows - count)
    lay_columns(lambda lanes: dv[2, :, :, lanes], laid, outer - first)
    lay_columns(lambda lanes: dv[1, :, :, lanes], laid, inner - first)
    if before is None:
        for x in range(2, rows - 2):
            lay_columns(lambda lanes: held[:, x - 1, :, lanes], laid, x - first)
    take_columns(
        sites, laid, lines, first, lambda line: jnp.zeros_like(lines[line, :]) if before is None else before[line, :]
    )
    for copy in stores(pl.ds(0, fields)):
        copy.wait()


def compiler_params(mib):
    return pltpu.CompilerParams(vmem_limit_bytes=mib * MIB)


def swapped(message, first, tiles):
    pairs = [(i, i + 1) for i in range(first, tiles - 1, 2)]
    return lax.ppermute(message, "tx", pairs + [(b, a) for a, b in pairs])


def shards(voltage, gating, recovery, tangents, parameters, region, fiber_class, electrode_site, electrode_owner):
    rows, levels, width = voltage.shape
    fields = tangents.shape[0]
    tiles = lax.axis_size("tx")
    f32 = jnp.float32
    smem = pl.BlockSpec(memory_space=pltpu.SMEM)
    hbm = pl.BlockSpec(memory_space=pl.ANY)
    vmem = pl.BlockSpec(memory_space=pltpu.VMEM)
    row = (levels, width)
    slots, depth = tiles * CAP, fields * levels
    linked = (lax.axis_index("tx") % 2).astype(jnp.int32)
    link_side, chip_side = linked.reshape(1), (1 - linked).reshape(1)

    message = jax.ShapeDtypeStruct((2 * fields + 2,) + row, f32)
    over_link = pl.pallas_call(
        message_kernel,
        out_shape=message,
        in_specs=[smem, smem] + [hbm] * 5,
        out_specs=hbm,
        scratch_shapes=[
            pltpu.VMEM(message.shape, f32),
            pltpu.VMEM((fields,) + row, f32),
            pltpu.VMEM((2, fields) + row, f32),
            pltpu.VMEM(row, f32),
            pltpu.VMEM((2,) + row, jnp.int32),
            pltpu.VMEM((8,) + row, f32),
            pltpu.SemaphoreType.DMA((12,)),
            pltpu.SemaphoreType.DMA((4,)),
        ],
        compiler_params=compiler_params(MESSAGE_MIB),
        cost_estimate=pl.CostEstimate(flops=1_000_000_000, bytes_accessed=MIB, transcendentals=0),
        name="message",
    )(link_side, parameters, tangents, voltage, gating, region, fiber_class)
    from_link = swapped(over_link, 1, tiles)

    owners = electrode_owner[:, 0]
    order = jnp.arange(owners.shape[0], dtype=jnp.int32)
    same = (owners[:, None] == owners[None, :]) & (order[:, None] < order[None, :])
    target = owners * CAP + jnp.sum(same.astype(jnp.int32), axis=0)
    sites = jnp.max(
        jnp.where(target[:, None] == jnp.arange(slots, dtype=jnp.int32)[None, :], electrode_site[:, None], -1), axis=0
    )

    field = pl.BlockSpec((rows,) + row, lambda i: (0, 0, 0))
    tan_spec = pl.BlockSpec((CHUNK, 3, rows) + row, lambda i: (i, 0, 0, 0, 0))
    tile = (rows,) + row
    partial_out, state, base_state, held, now, later, rest = pl.pallas_call(
        main_kernel,
        grid=(fields // CHUNK,),
        out_shape=(
            jax.ShapeDtypeStruct(tangents.shape, f32),
            jax.ShapeDtypeStruct((2, 3, fields) + row, f32),
            jax.ShapeDtypeStruct((2, 12) + row, f32),
            jax.ShapeDtypeStruct((fields, rows - 2) + row, f32),
            jax.ShapeDtypeStruct((fields,) + row, f32),
            jax.ShapeDtypeStruct((fields,) + row, f32),
            jax.ShapeDtypeStruct((2,) + row, f32),
        ),
        in_specs=[smem, smem] + [field] * 5 + [hbm],
        out_specs=(
            tan_spec,
            pl.BlockSpec((2, 3, CHUNK) + row, lambda i: (0, 0, i, 0, 0)),
            pl.BlockSpec((2, 12) + row, lambda i: (0, 0, 0, 0)),
            pl.BlockSpec((CHUNK, rows - 2) + row, lambda i: (i, 0, 0, 0)),
            pl.BlockSpec((CHUNK,) + row, lambda i: (i, 0, 0)),
            pl.BlockSpec((CHUNK,) + row, lambda i: (i, 0, 0)),
            pl.BlockSpec((2,) + row, lambda i: (0, 0, 0)),
        ),
        scratch_shapes=[
            pltpu.VMEM((5,) + tile, f32),
            pltpu.VMEM((4,) + tile, f32),
            pltpu.VMEM((4,) + tile, f32),
            pltpu.VMEM((CHUNK,) + tile, f32),
            pltpu.VMEM((CHUNK,) + tile, f32),
            pltpu.VMEM((CHUNK,) + tile, f32),
            pltpu.VMEM((2, CHUNK, 3, rows) + row, f32),
            pltpu.SemaphoreType.DMA((2,)),
        ],
        compiler_params=compiler_params(INTERIOR_MIB),
        cost_estimate=pl.CostEstimate(flops=1000, bytes_accessed=1024, transcendentals=0),
        name="interior",
    )(chip_side, parameters, voltage, gating, recovery, region, fiber_class, tangents)
    from_chip = tuple(swapped(part, 0, tiles) for part in (now, later, rest))

    def tail(side_at, filled, *messages):
        return pl.pallas_call(
            tail_kernel,
            out_shape=(jax.ShapeDtypeStruct(tangents.shape, f32), jax.ShapeDtypeStruct((slots, depth), f32)),
            in_specs=[smem, smem] + [vmem] * 3 + [hbm] + [vmem] * len(messages),
            out_specs=(hbm, vmem),
            scratch_shapes=[
                pltpu.VMEM((3, fields) + row, f32),
                pltpu.VMEM((fields,) + row, f32),
                pltpu.VMEM((fields,) + row, f32),
                pltpu.VMEM((2 if len(messages) == 3 else rows - 2, width, depth), f32),
                pltpu.VMEM((7,) + row, f32),
                pltpu.SemaphoreType.DMA((4,)),
            ],
            input_output_aliases={5: 0},
            compiler_params=compiler_params(20),
            cost_estimate=pl.CostEstimate(flops=1000, bytes_accessed=1024, transcendentals=0),
            name="tail",
        )(side_at, sites, state, base_state, held, filled, *messages)

    filled, lines = tail(chip_side, partial_out, now, later, *from_chip)
    from_link, lines = lax.optimization_barrier((from_link, lines))
    tangents_out, outgoing = tail(link_side, filled, over_link, from_link, lines)

    arrived = lax.all_to_all(outgoing.reshape(tiles, CAP, depth), "tx", split_axis=0, concat_axis=0, tiled=True)
    return tangents_out, arrived.reshape(slots, depth)


def solution(mesh):
    line = P(("groups", "tx"), None, None)
    placed = (
        line,
        line,
        line,
        P(None, None, ("groups", "tx"), None, None),
        P("groups"),
        line,
        line,
        P(("groups", "tx")),
        P(("groups", "tx"), None),
    )
    return jax.shard_map(
        shards,
        mesh=mesh,
        in_specs=placed,
        out_specs=(P(None, None, ("groups", "tx"), None, None), P(("groups", "tx"), None)),
        check_vma=False,
    )
```

```python
import functools

import jax
import jax.numpy as jnp
from jax import lax
from jax.experimental import pallas as pl
from jax.experimental.pallas import tpu as pltpu
from jax.sharding import PartitionSpec as P

CAP = 16
GROUP = 8
LANES = 128
CHUNK = 2
WIDE = 1
MESSAGE_MIB = 54
INTERIOR_MIB = 36
MIB = 1 << 20

CENTRE = 0.7
DEPTH = 0.025


def rolled(x, shift, axis):
    return pltpu.roll(x, shift % x.shape[axis], axis)


def stencil_coeffs(fiber):
    width = fiber.shape[-1]
    x_coef = jnp.where(fiber == 0, 0.1, jnp.where(fiber == 2, 0.025, 0.0625))
    y_coef = 0.125 - x_coef
    w_coef = jnp.where(fiber == 1, 0.01875, jnp.where(fiber == 3, -0.01875, 0.0))
    return (x_coef,) + shifted_pair(y_coef, width) + shifted_pair(w_coef, width)


def shifted_pair(coef, width):
    lane = lax.broadcasted_iota(jnp.int32, coef.shape, 1)
    before = jnp.where(lane == 0, 0.0, rolled(coef, 1, 1))
    after = jnp.where(lane == width - 1, 0.0, rolled(coef, -1, 1))
    return before, after


def depth_sum(levels_of, k, count):
    u = levels_of(k)
    level = lax.broadcasted_iota(jnp.int32, u.shape, 0)
    first = u if k == 0 else rolled(levels_of(k - 1), 1, 0)
    last = u if k == count - 1 else rolled(levels_of(k + 1), -1, 0)
    return jnp.where(level == 0, first, rolled(u, 1, 0)) + jnp.where(level == GROUP - 1, last, rolled(u, -1, 0))


def plane(u, outside, inside, coeffs):
    x_coef, y_before, y_after, w_before, w_after = coeffs
    if outside is None:
        total, gap = inside, -inside
    else:
        total, gap = outside + inside, outside - inside
    return (
        x_coef * total
        + rolled(y_before * u + w_before * gap, -1, 1)
        + rolled(y_after * u - w_after * gap, 1, 1)
    )


def one_sided(u, x_coef, w_before, w_after):
    return x_coef * u + rolled(w_before * u, -1, 1) - rolled(w_after * u, 1, 1)


def signed(coeffs, sign):
    x_coef, y_before, y_after, w_before, w_after = coeffs
    return x_coef, y_before, y_after, sign * w_before, sign * w_after


def local_gain(region, params):
    gain = jnp.zeros(region.shape, jnp.float32)
    for p in range(params.shape[0]):
        gain = jnp.where(region == p, params[p], gain)
    return 0.2 * gain


def reaction(v, h, gain):
    current = v - v * v * v * (1.0 / 3.0)
    slope = 1.0 - v * v
    gate = 1.0 / (1.0 + jnp.exp(-4.0 * v))
    of_v = CENTRE + gain * h * slope
    return of_v, gain * current, 0.2 * h * current, gate * (1.0 - gate), gate, gain * h * current


def groups_of(levels):
    return [(k, pl.ds(GROUP * k, GROUP)) for k in range(levels // GROUP)]


def edge_of(side, rows):
    return side * (rows - 1), 1 + side * (rows - 3), (2 * side - 1).astype(jnp.float32)


def message_kernel(side_at, params, tan, v, h, reg, fib, sent, out, dv, dhc, base, label, coef, sems, sent_sems):
    fields, rows = tan.shape[0], tan.shape[2]
    groups = groups_of(tan.shape[3])
    outer, inner, sign = edge_of(side_at[0], rows)
    half = fields // 4
    pairs = [
        (v.at[outer], out.at[2 * fields]),
        (h.at[outer], base),
        (reg.at[outer], label.at[0]),
        (fib.at[outer], label.at[1]),
    ]
    for at in range(0, fields, half):
        part = pl.ds(at, half)
        pairs += [
            (tan.at[part, 0, outer], out.at[part]),
            (tan.at[part, 0, inner], dv.at[part]),
            (tan.at[part, 1, outer], dhc.at[0, part]),
            (tan.at[part, 2, outer], dhc.at[1, part]),
        ]
    copies = [pltpu.make_async_copy(a, b, sems.at[k]) for k, (a, b) in enumerate(pairs)]
    for copy in copies:
        copy.start()

    def send(first, count, k):
        part = pl.ds(first, count)
        return pltpu.make_async_copy(out.at[part], sent.at[part], sent_sems.at[k])

    for copy in copies[:4]:
        copy.wait()
    for _, z in groups:
        fiber = label[1, z]
        gain = local_gain(label[0, z], params)
        of_v, of_h, of_m, _, _, _ = reaction(out[2 * fields, z], base[z], gain)
        for i, value in enumerate(signed(stencil_coeffs(fiber), sign) + (of_v, of_h, of_m)):
            coef[i, z] = value
        out[2 * fields + 1, z] = (fiber + 1).astype(jnp.float32)
    send(2 * fields, 2, 0).start()

    for at in range(4):
        for copy in copies[4 + 4 * at : 8 + 4 * at]:
            copy.wait()
        send(at * half, half, 1 + at).start()

        @pl.loop(at * half // CHUNK, (at + 1) * half // CHUNK)
        def _(step):
            for k, z in groups:
                coeffs = tuple(coef[i, z] for i in range(5))
                for j in range(CHUNK):
                    p = step * CHUNK + j
                    u = out[p, z]
                    out[fields + p, z] = (
                        coef[5, z] * u
                        + plane(u, None, dv[p, z], coeffs)
                        + DEPTH * depth_sum(lambda i: out[p, groups[i][1]], k, len(groups))
                        + coef[6, z] * dhc[0, p, z]
                        + jnp.where(label[0, z] == p, coef[7, z], 0.0)
                        - 0.1 * dhc[1, p, z]
                    )
            send(fields + step * CHUNK, CHUNK, 5).start()

    send(2 * fields, 2, 0).wait()
    for at in range(4):
        send(at * half, half, 1 + at).wait()
    send(fields, fields, 5).wait()


def main_kernel(
    side_at, params, v, h, c, reg, fib, tan_all, out, state, base_state, held, now, later, rest,
    coef, gate_1, gate_2, dv, dh, dc, slots, sems
):
    step = pl.program_id(0)
    rows, levels, _ = v.shape
    chip_outer, _, _ = edge_of(side_at[0], rows)
    chunk, count = CHUNK, pl.num_programs(0)
    groups = groups_of(levels)
    ends = ((0, 0), (1, rows - 1))
    tan = slots.at[step % 2]

    def load(at, slot):
        return pltpu.make_async_copy(tan_all.at[pl.ds(at * chunk, chunk)], slots.at[slot], sems.at[slot])

    @pl.when(step == 0)
    def _():
        for slot in range(2):
            load(slot, slot).start()

    @pl.when(step == 0)
    def _():
        def base(x, low, high, side):
            for k, z in groups:
                coeffs = stencil_coeffs(fib[x, z])
                gain = local_gain(reg[x, z], params)
                u = v[x, z]
                of_v, of_h, of_m, of_g, gate, push = reaction(u, h[x, z], gain)
                if side is not None:
                    coeffs = signed(coeffs, 2.0 * side - 1.0)
                for i in range(5):
                    coef[i, x, z] = coeffs[i]
                for i, value in enumerate((of_v, of_h, of_m, of_g)):
                    gate_1[i, x, z] = value
                depth = depth_sum(lambda i: v[x, groups[i][1]], k, len(groups))
                around = plane(u, v[high, z] if side is None else None, v[low, z], coeffs)
                u_new = CENTRE * u + around + DEPTH * depth + push - 0.1 * c[x, z]
                h_new = 0.75 * h[x, z] + 0.25 * gate
                if side is None:
                    for i, value in enumerate(reaction(u_new, h_new, gain)[:4]):
                        gate_2[i, x, z] = value
                else:
                    values = coeffs + (u_new, h_new, gain, reg[x, z].astype(jnp.float32))
                    for i, value in enumerate(values):
                        base_state[side, i, z] = value

        pl.loop(1, rows - 1)(lambda x: base(x, x - 1, x + 1, None))
        base(0, 1, None, 0)
        base(rows - 1, rows - 2, None, 1)
        for side, x in ((0, 1), (1, rows - 2)):
            base_state[side, 9] = coef[0, x]
            base_state[side, 10] = (2.0 * side - 1.0) * coef[3, x]
            base_state[side, 11] = (2.0 * side - 1.0) * coef[4, x]
        rest[0] = v[chip_outer]
        rest[1] = (fib[chip_outer] + 1).astype(jnp.float32)

    load(step, step % 2).wait()
    for side, x in ends:
        inside = 1 if side == 0 else rows - 2
        for k, z in groups:
            coeffs = tuple(coef[i, x, z] for i in range(5))
            for j in range(chunk):
                u = tan[j, 0, x, z]
                dv[j, x, z] = (
                    gate_1[0, x, z] * u
                    + plane(u, None, tan[j, 0, inside, z], coeffs)
                    + DEPTH * depth_sum(lambda i: tan[j, 0, x, groups[i][1]], k, len(groups))
                    + gate_1[1, x, z] * tan[j, 1, x, z]
                    + jnp.where(reg[x, z] == step * chunk + j, gate_1[2, x, z], 0.0)
                    - 0.1 * tan[j, 2, x, z]
                )
                state[side, 0, j, z] = 0.75 * tan[j, 1, x, z] + gate_1[3, x, z] * u
                state[side, 1, j, z] = 0.096 * tan[j, 2, x, z] + 0.005 * u
    for j in range(chunk):
        now[j] = tan[j, 0, chip_outer]
        later[j] = dv[j, chip_outer]

    def step_1(x):
        for k, z in groups:
            coeffs = tuple(coef[i, x, z] for i in range(5))
            for j in range(chunk):
                u = tan[j, 0, x, z]
                dv[j, x, z] = (
                    gate_1[0, x, z] * u
                    + plane(u, tan[j, 0, x + 1, z], tan[j, 0, x - 1, z], coeffs)
                    + DEPTH * depth_sum(lambda i: tan[j, 0, x, groups[i][1]], k, len(groups))
                    + gate_1[1, x, z] * tan[j, 1, x, z]
                    + jnp.where(reg[x, z] == step * chunk + j, gate_1[2, x, z], 0.0)
                    - 0.1 * tan[j, 2, x, z]
                )
                dh[j, x, z] = 0.75 * tan[j, 1, x, z] + gate_1[3, x, z] * u
                dc[j, x, z] = 0.096 * tan[j, 2, x, z] + 0.005 * u

    pl.loop(1, rows - 1)(step_1)

    @pl.when(step + 2 < count)
    def _():
        load(step + 2, step % 2).start()

    def step_2(x):
        for k, z in groups:
            coeffs = tuple(coef[i, x, z] for i in range(5))
            for j in range(chunk):
                u = dv[j, x, z]
                new = (
                    gate_2[0, x, z] * u
                    + plane(u, dv[j, x + 1, z], dv[j, x - 1, z], coeffs)
                    + DEPTH * depth_sum(lambda i: dv[j, x, groups[i][1]], k, len(groups))
                    + gate_2[1, x, z] * dh[j, x, z]
                    + jnp.where(reg[x, z] == step * chunk + j, gate_2[2, x, z], 0.0)
                    - dc[j, x, z]
                )
                out[j, 0, x, z] = new
                held[j, x - 1, z] = new
                out[j, 1, x, z] = 0.75 * dh[j, x, z] + gate_2[3, x, z] * u
                out[j, 2, x, z] = 9.6 * dc[j, x, z] + 0.05 * u

    pl.loop(1, rows - 1)(step_2)
    for side, x in ((0, 1), (1, rows - 2)):
        for j in range(chunk):
            state[side, 2, j] = dv[j, x]


def lay_columns(rows_of, laid, index):
    for at in range(laid.shape[1] // LANES):
        lanes = pl.ds(at * LANES, LANES)
        laid[index, lanes, :] = rows_of(lanes).reshape(LANES, LANES).T


def take_columns(sites, laid, out, first, other):
    count, width, depth = laid.shape
    flat = laid.reshape(count * width, depth)

    def take(s, carry):
        place = sites[s] - first * width
        here = (sites[s] >= 0) & (place >= 0) & (place < count * width)
        line = pl.ds(s, 1)
        out[line, :] = jnp.where(here, flat[pl.ds(jnp.where(here, place, 0), 1), :], other(line))
        return carry

    lax.fori_loop(0, out.shape[0], take, 0, unroll=8)


def tail_kernel(side_at, sites, state, base_state, held, _, *refs):
    out, lines, dv, dh, dc, laid, coef, sems = refs[-8:]
    fields, levels, width = dv.shape[1:]
    if len(refs) == 11:
        own, there, before = refs[:3]
        now, later = own.at[pl.ds(0, fields)], own.at[pl.ds(fields, fields)]
        far_now, far_later, far_rest = (there.at[pl.ds(i * fields, fields if i < 2 else 2)] for i in range(3))
    else:
        now, later, far_now, far_later, far_rest = refs[:5]
        before = None
    rows = out.shape[2]
    groups = groups_of(levels)
    side = side_at[0]
    outer, inner, sign = edge_of(side, rows)

    for _, z in groups:
        v_new = base_state[side, 5, z] + one_sided(far_rest[0, z], *(base_state[side, i, z] for i in (0, 3, 4)))
        for i, value in enumerate(reaction(v_new, base_state[side, 6, z], base_state[side, 7, z])[:4]):
            coef[i, z] = value
        sent = far_rest[1, z]
        far = signed(stencil_coeffs((sent - 1.0).astype(jnp.int32)), -sign)
        for i, at in enumerate((0, 3, 4)):
            coef[4 + i, z] = jnp.where(sent > 0.5, far[at], 0.0)

    def stores(part):
        pairs = ((dv.at[2], 0, outer), (dv.at[1], 0, inner), (dh, 1, outer), (dc, 2, outer))
        return [pltpu.make_async_copy(a.at[part], out.at[part, f, x], sems.at[i]) for i, (a, f, x) in enumerate(pairs)]

    @pl.loop(0, fields // WIDE)
    def _(step):
        for k, z in groups:
            own_row = tuple(base_state[side, i, z] for i in (0, 3, 4))
            next_row = tuple(base_state[side, 9 + i, z] for i in range(3))
            for j in range(WIDE):
                p = step * WIDE + j
                extra = one_sided(far_now[p, z], *own_row)
                dv[0, p, z] = later[p, z] + extra
                dv[1, p, z] = held[p, inner - 1, z] + one_sided(extra, *next_row)
        for k, z in groups:
            coeffs = tuple(base_state[side, i, z] for i in range(5))
            far = tuple(coef[i, z] for i in (4, 5, 6))
            for j in range(WIDE):
                p = step * WIDE + j
                u = dv[0, p, z]
                outside = far_later[p, z] + one_sided(now[p, z], *far)
                dv[2, p, z] = (
                    coef[0, z] * u
                    + plane(u, outside, state[side, 2, p, z], coeffs)
                    + DEPTH * depth_sum(lambda i: dv[0, p, groups[i][1]], k, len(groups))
                    + coef[1, z] * state[side, 0, p, z]
                    + jnp.where(base_state[side, 8, z] == p.astype(jnp.float32), coef[2, z], 0.0)
                    - state[side, 1, p, z]
                )
                dh[p, z] = 0.75 * state[side, 0, p, z] + coef[3, z] * u
                dc[p, z] = 9.6 * state[side, 1, p, z] + 0.05 * u

        for copy in stores(pl.ds(step * WIDE, WIDE)):
            copy.start()

    count = laid.shape[0]
    first = side * (rows - count)
    lay_columns(lambda lanes: dv[2, :, :, lanes], laid, outer - first)
    lay_columns(lambda lanes: dv[1, :, :, lanes], laid, inner - first)
    if before is None:
        for x in range(2, rows - 2):
            lay_columns(lambda lanes: held[:, x - 1, :, lanes], laid, x - first)
    take_columns(
        sites, laid, lines, first, lambda line: jnp.zeros_like(lines[line, :]) if before is None else before[line, :]
    )
    for copy in stores(pl.ds(0, fields)):
        copy.wait()


def compiler_params(mib):
    return pltpu.CompilerParams(vmem_limit_bytes=mib * MIB)


def swapped(message, first, tiles):
    pairs = [(i, i + 1) for i in range(first, tiles - 1, 2)]
    return lax.ppermute(message, "tx", pairs + [(b, a) for a, b in pairs])


def shards(voltage, gating, recovery, tangents, parameters, region, fiber_class, electrode_site, electrode_owner):
    rows, levels, width = voltage.shape
    fields = tangents.shape[0]
    tiles = lax.axis_size("tx")
    f32 = jnp.float32
    smem = pl.BlockSpec(memory_space=pltpu.SMEM)
    hbm = pl.BlockSpec(memory_space=pl.ANY)
    vmem = pl.BlockSpec(memory_space=pltpu.VMEM)
    row = (levels, width)
    slots, depth = tiles * CAP, fields * levels
    linked = (lax.axis_index("tx") % 2).astype(jnp.int32)
    link_side, chip_side = linked.reshape(1), (1 - linked).reshape(1)

    message = jax.ShapeDtypeStruct((2 * fields + 2,) + row, f32)
    over_link = pl.pallas_call(
        message_kernel,
        out_shape=message,
        in_specs=[smem, smem] + [hbm] * 5,
        out_specs=hbm,
        scratch_shapes=[
            pltpu.VMEM(message.shape, f32),
            pltpu.VMEM((fields,) + row, f32),
            pltpu.VMEM((2, fields) + row, f32),
            pltpu.VMEM(row, f32),
            pltpu.VMEM((2,) + row, jnp.int32),
            pltpu.VMEM((8,) + row, f32),
            pltpu.SemaphoreType.DMA((20,)),
            pltpu.SemaphoreType.DMA((6,)),
        ],
        compiler_params=compiler_params(MESSAGE_MIB),
        cost_estimate=pl.CostEstimate(flops=1_000_000_000, bytes_accessed=MIB, transcendentals=0),
        name="message",
    )(link_side, parameters, tangents, voltage, gating, region, fiber_class)
    from_link = swapped(over_link, 1, tiles)

    owners = electrode_owner[:, 0]
    order = jnp.arange(owners.shape[0], dtype=jnp.int32)
    same = (owners[:, None] == owners[None, :]) & (order[:, None] < order[None, :])
    target = owners * CAP + jnp.sum(same.astype(jnp.int32), axis=0)
    sites = jnp.max(
        jnp.where(target[:, None] == jnp.arange(slots, dtype=jnp.int32)[None, :], electrode_site[:, None], -1), axis=0
    )

    field = pl.BlockSpec((rows,) + row, lambda i: (0, 0, 0))
    tan_spec = pl.BlockSpec((CHUNK, 3, rows) + row, lambda i: (i, 0, 0, 0, 0))
    tile = (rows,) + row
    partial_out, state, base_state, held, now, later, rest = pl.pallas_call(
        main_kernel,
        grid=(fields // CHUNK,),
        out_shape=(
            jax.ShapeDtypeStruct(tangents.shape, f32),
            jax.ShapeDtypeStruct((2, 3, fields) + row, f32),
            jax.ShapeDtypeStruct((2, 12) + row, f32),
            jax.ShapeDtypeStruct((fields, rows - 2) + row, f32),
            jax.ShapeDtypeStruct((fields,) + row, f32),
            jax.ShapeDtypeStruct((fields,) + row, f32),
            jax.ShapeDtypeStruct((2,) + row, f32),
        ),
        in_specs=[smem, smem] + [field] * 5 + [hbm],
        out_specs=(
            tan_spec,
            pl.BlockSpec((2, 3, CHUNK) + row, lambda i: (0, 0, i, 0, 0)),
            pl.BlockSpec((2, 12) + row, lambda i: (0, 0, 0, 0)),
            pl.BlockSpec((CHUNK, rows - 2) + row, lambda i: (i, 0, 0, 0)),
            pl.BlockSpec((CHUNK,) + row, lambda i: (i, 0, 0)),
            pl.BlockSpec((CHUNK,) + row, lambda i: (i, 0, 0)),
            pl.BlockSpec((2,) + row, lambda i: (0, 0, 0)),
        ),
        scratch_shapes=[
            pltpu.VMEM((5,) + tile, f32),
            pltpu.VMEM((4,) + tile, f32),
            pltpu.VMEM((4,) + tile, f32),
            pltpu.VMEM((CHUNK,) + tile, f32),
            pltpu.VMEM((CHUNK,) + tile, f32),
            pltpu.VMEM((CHUNK,) + tile, f32),
            pltpu.VMEM((2, CHUNK, 3, rows) + row, f32),
            pltpu.SemaphoreType.DMA((2,)),
        ],
        compiler_params=compiler_params(INTERIOR_MIB),
        cost_estimate=pl.CostEstimate(flops=1000, bytes_accessed=1024, transcendentals=0),
        name="interior",
    )(chip_side, parameters, voltage, gating, recovery, region, fiber_class, tangents)
    from_chip = tuple(swapped(part, 0, tiles) for part in (now, later, rest))

    def tail(side_at, filled, *messages):
        return pl.pallas_call(
            tail_kernel,
            out_shape=(jax.ShapeDtypeStruct(tangents.shape, f32), jax.ShapeDtypeStruct((slots, depth), f32)),
            in_specs=[smem, smem] + [vmem] * 3 + [hbm] + [vmem] * len(messages),
            out_specs=(hbm, vmem),
            scratch_shapes=[
                pltpu.VMEM((3, fields) + row, f32),
                pltpu.VMEM((fields,) + row, f32),
                pltpu.VMEM((fields,) + row, f32),
                pltpu.VMEM((2 if len(messages) == 3 else rows - 2, width, depth), f32),
                pltpu.VMEM((7,) + row, f32),
                pltpu.SemaphoreType.DMA((4,)),
            ],
            input_output_aliases={5: 0},
            compiler_params=compiler_params(20),
            cost_estimate=pl.CostEstimate(flops=1000, bytes_accessed=1024, transcendentals=0),
            name="tail",
        )(side_at, sites, state, base_state, held, filled, *messages)

    filled, lines = tail(chip_side, partial_out, now, later, *from_chip)
    from_link, lines = lax.optimization_barrier((from_link, lines))
    tangents_out, outgoing = tail(link_side, filled, over_link, from_link, lines)

    arrived = lax.all_to_all(outgoing.reshape(tiles, CAP, depth), "tx", split_axis=0, concat_axis=0, tiled=True)
    return tangents_out, arrived.reshape(slots, depth)


def solution(mesh):
    line = P(("groups", "tx"), None, None)
    placed = (
        line,
        line,
        line,
        P(None, None, ("groups", "tx"), None, None),
        P("groups"),
        line,
        line,
        P(("groups", "tx")),
        P(("groups", "tx"), None),
    )
    return jax.shard_map(
        shards,
        mesh=mesh,
        in_specs=placed,
        out_specs=(P(None, None, ("groups", "tx"), None, None), P(("groups", "tx"), None)),
        check_vma=False,
    )
```
